32 devices in a mesh: state: 8 (over y, x, core), mesh: 4 (over z).
Axes of the slice: x: 2, y: 2, z: 4, core: 2. Of those that a mesh axis runs over, the one named last changes fastest.
Arguments:
- states_in: float32 [5508, 4096], P('mesh', 'state'), may hold values from -6 to 6
- rotation: float32 [4096, 4096], P(None, 'state'), may hold values from -0.09375 to 0.09375
- stiffness: float32 [4, 729, 729], P('mesh'), as said below
- potential: float32 [5508], P('mesh'), may hold values from -1 to 1
- cell_nodes: int32 [8, 729], P('mesh'), may hold values from 0 to 1376, as said below
- shared_rows: int32 [16, 153], P('mesh'), may hold values from 0 to 1376, as said below
- shared_count: int32 [4, 4], P('mesh'), may hold values from 0 to 153, as said below
Outputs:
- filtered: float32 [5508, 4096], P('mesh', 'state')
The draws below stay inside these ranges and needn't reach their ends.
Inputs may be any that keep to these rules, and one draw needn't show every extreme that they name: `cell_nodes`: each partition's 2 cells name its 1377 local nodes as a row of hexahedral cells of order 8 sharing faces; every local node is named by some cell. `shared_rows`: used rows name the partition's nodes on the face toward the partner, in the same geometric order as the partner's matching list; rows beyond the count name arbitrary local nodes. `shared_count`: count s of partition p equals count s ^ 1 of its partner; for s = 0, 1 it is 0 or from 40 to 81, for s = 2, 3 it is 0 or from 76 to 153; it is 0 where the partner lies outside the G by G grid; count 2 of partition 0 is 153. `stiffness`: symmetric with a diagonal of 1 to 3.
All inputs are finite; a program needn't handle non-finite values.
Results may differ from the reference program's by a relative error of at most 0.0001.
Values sent between devices are 32-bit elements; how exact they have to be, the bound alone decides.
A program may use at most 128 MiB of HBM per device.

```python
import math
import jax
import jax.numpy as jnp
from jax import lax

NSTATE = 4096
ORDER = 8
CELLS = 2
CHEB = 2
NPC = 729
NODE_DEV = 1377
FACE_X = 81
SHARE_MAX = 153
NODES = 5508
N_MESH = 4


def mesh_layout(key):
    side = ORDER + 1
    grid_side = math.isqrt(N_MESH)
    keys = jax.random.split(jax.random.fold_in(key, 11), N_MESH)
    perms = jax.vmap(lambda sub: jax.random.permutation(sub, NODE_DEV))(keys).astype(jnp.int32)
    local = jnp.arange(NPC, dtype=jnp.int32)
    first = local // (side * side)
    second = local // side % side
    third = local % side
    cellidx = jnp.arange(CELLS, dtype=jnp.int32)[:, None]
    structure = ((cellidx * ORDER + first[None, :]) * side + second[None, :]) * side + third[None, :]
    nodes = perms[:, structure].reshape(N_MESH * CELLS, NPC)
    face_rows = jnp.arange(FACE_X, dtype=jnp.int32)
    far_x = CELLS * ORDER
    face_high = (far_x * side + face_rows // side) * side + face_rows % side
    face_low = face_rows // side * side + face_rows % side
    pad = jnp.zeros((SHARE_MAX - FACE_X,), jnp.int32)
    face_high = jnp.concatenate([face_high, pad])
    face_low = jnp.concatenate([face_low, pad])
    long_rows = jnp.arange(SHARE_MAX, dtype=jnp.int32)
    side_high = (long_rows // side * side + ORDER) * side + long_rows % side
    side_low = long_rows // side * side * side + long_rows % side
    lists = jnp.stack([face_high, face_low, side_high, side_low])
    rows = perms[:, lists].reshape(N_MESH * 4, SHARE_MAX)
    parts = jnp.arange(N_MESH, dtype=jnp.int32)
    place_a = parts // grid_side
    place_b = parts % grid_side
    link_a = jax.random.randint(jax.random.fold_in(key, 23), (N_MESH,), 0, 4) < 3
    link_b = jax.random.randint(jax.random.fold_in(key, 29), (N_MESH,), 0, 4) < 3
    link_b = link_b | (parts == 0)
    size_a = jax.random.randint(jax.random.fold_in(key, 31), (N_MESH,), FACE_X // 2, FACE_X + 1)
    size_b = jax.random.randint(jax.random.fold_in(key, 43), (N_MESH,), SHARE_MAX // 2, SHARE_MAX + 1)
    size_b = jnp.where(parts == 0, SHARE_MAX, size_b)
    count_zero = jnp.where((place_a < grid_side - 1) & link_a, size_a, 0)
    count_two = jnp.where((place_b < grid_side - 1) & link_b, size_b, 0)
    count_one = jnp.roll(count_zero, grid_side)
    count_one = jnp.where(place_a > 0, count_one, 0)
    count_three = jnp.roll(count_two, 1)
    count_three = jnp.where(place_b > 0, count_three, 0)
    counts = jnp.stack([count_zero, count_one, count_two, count_three], axis=1).astype(jnp.int32)
    return (nodes, rows, counts)


def draw_cell_nodes(key, part):
    return mesh_layout(key)[0]


def draw_shared_rows(key, part):
    return mesh_layout(key)[1]


def draw_shared_count(key, part):
    return mesh_layout(key)[2]


def draw_stiffness(key, part):
    inner = jax.random.fold_in(key, 37)
    raw = jax.random.normal(inner, (N_MESH, NPC, NPC), jnp.float32)
    offdiag = (raw + jnp.swapaxes(raw, 1, 2)) * (0.7 / math.sqrt(NPC))
    diag_vals = jax.random.uniform(jax.random.fold_in(key, 41), (N_MESH, NPC), jnp.float32, 1.0, 3.0)
    unit = jnp.eye(NPC, dtype=jnp.float32)
    return offdiag * (1.0 - unit)[None] + unit[None] * diag_vals[:, :, None]


def block_levels(stream_key, extent, shards, low, high):
    loudness = 1.0
    for dim, blocks in shards:
        heights = jax.random.uniform(jax.random.fold_in(jax.random.fold_in(stream_key, 6), dim), (blocks,), jnp.float32, low / len(shards), high / len(shards))
        loudness = loudness * jnp.repeat(jnp.exp(heights), extent[dim] // blocks).reshape((-1,) + (1,) * (len(extent) - 1 - dim))
    return loudness


def bell_draw(key, dims, spread, most, pieces=(), kind=jnp.bfloat16):
    array = jax.random.normal(key, dims, jnp.float32) * spread
    if len(pieces) > 0:
        array = block_levels(key, dims, pieces, -0.22, 0.18) * array
    return jnp.clip(array, min=-most, max=most).astype(kind)


def setup_inputs(seed: int = 0) -> dict:
    key_of = jax.random.split(jax.random.key(seed), 8)
    return {
        "states_in": bell_draw(key_of[0], (NODES, NSTATE), 1.0, 6.0, ((0, 4), (1, 8)), jnp.float32),
        "rotation": bell_draw(key_of[1], (NSTATE, NSTATE), NSTATE ** -0.5, 0.09375, ((1, 8),), jnp.float32),
        "stiffness": draw_stiffness(jax.random.fold_in(key_of[7], 71), 0),
        "potential": jnp.clip(jax.random.uniform(key_of[3], (NODES,), jnp.float32, -1.0, 1.0) * block_levels(key_of[3], (NODES,), ((0, 4),), -0.4, 0.0), -1.0, 1.0),
        "cell_nodes": draw_cell_nodes(jax.random.fold_in(key_of[7], 71), 0),
        "shared_rows": draw_shared_rows(jax.random.fold_in(key_of[7], 71), 0),
        "shared_count": draw_shared_count(jax.random.fold_in(key_of[7], 71), 0),
    }


center_shift = 3.0
half_width = 4.0

def apply_cells(field, stiffness, nodes):

    def single(packed):
        values, matrix, index = packed
        gathered = values[index]
        product = jnp.einsum('ij,cjs->cis', matrix, gathered, precision=lax.Precision.HIGHEST)
        return jnp.zeros_like(values).at[index.reshape(-1)].add(product.reshape(-1, values.shape[1]))
    return lax.map(single, (field, stiffness, nodes))

def pick_rows(values, rows, mask, slot):
    return jax.vmap(lambda vals, idx, msk: vals[idx[slot]] * msk[slot][:, None])(values, rows, mask)

def put_rows(values, rows, slot, got):
    return jax.vmap(lambda vals, idx, add: vals.at[idx[slot]].add(add))(values, rows, got)

def operator(field, stiffness, potential, nodes, rows, mask, grid_side):
    local = apply_cells(field, stiffness, nodes)
    send_one = pick_rows(local, rows, mask, 1)
    send_zero = pick_rows(local, rows, mask, 0)
    from_next = jnp.roll(send_one, -grid_side, axis=0) * mask[:, 0, :, None]
    from_prev = jnp.roll(send_zero, grid_side, axis=0) * mask[:, 1, :, None]
    sectioned = put_rows(put_rows(local, rows, 0, from_next), rows, 1, from_prev)
    send_three = pick_rows(sectioned, rows, mask, 3)
    send_two = pick_rows(sectioned, rows, mask, 2)
    from_right = jnp.roll(send_three, -1, axis=0) * mask[:, 2, :, None]
    from_left = jnp.roll(send_two, 1, axis=0) * mask[:, 3, :, None]
    assembled = put_rows(put_rows(sectioned, rows, 2, from_right), rows, 3, from_left)
    return assembled + potential[:, :, None] * field

def reference(states_in, rotation, stiffness, potential, cell_nodes, shared_rows, shared_count):
    rotated = jnp.dot(states_in, rotation, precision=lax.Precision.HIGHEST, preferred_element_type=jnp.float32)
    grid_side = math.isqrt(N_MESH)
    field = rotated.reshape(N_MESH, NODE_DEV, NSTATE)
    pot = potential.reshape(N_MESH, NODE_DEV)
    nodes = cell_nodes.reshape(N_MESH, CELLS, NPC)
    rows = shared_rows.reshape(N_MESH, 4, SHARE_MAX)
    mask = (jnp.arange(SHARE_MAX)[None, None, :] < shared_count[:, :, None]).astype(jnp.float32)
    previous = field
    current = (operator(field, stiffness, pot, nodes, rows, mask, grid_side) - center_shift * field) / half_width
    for step_index in range(1, CHEB):
        applied = operator(current, stiffness, pot, nodes, rows, mask, grid_side)
        following = 2.0 * (applied - center_shift * current) / half_width - previous
        previous = current
        current = following
    return current.reshape(NODES, NSTATE)
```

```python
import functools
import math

import jax
import jax.numpy as jnp
from jax import lax
from jax.experimental import pallas as pl
from jax.experimental.pallas import tpu as pltpu
from jax.sharding import PartitionSpec as P

center_shift = 3.0
half_width = 4.0
f32 = jnp.float32
bf16 = jnp.bfloat16
MESH = pl.DeviceIdType.MESH


def from_behind(value, axis, steps):
    count = lax.axis_size(axis)
    first, last = (max(0, -steps), min(count, count - steps))
    return lax.ppermute(value, axis, [(source, source + steps) for source in range(first, last)])


def matmul(left, right):
    return jnp.dot(left, right, precision=lax.Precision.HIGHEST, preferred_element_type=jnp.float32)


def per_device(states_in, rotation, stiffness, potential, cell_nodes, shared_rows, shared_count):
    block_cols = states_in.shape[1]
    rotated = matmul(lax.all_gather(states_in, "state", axis=1, tiled=True), rotation)
    grid_side = math.isqrt(lax.axis_size("mesh"))
    row_mask = (jnp.arange(shared_rows.shape[1])[None, :] < shared_count[0][:, None]).astype(
        jnp.float32
    )

    def trade(values, send_slot, recv_slot, offset):
        block = values[shared_rows[send_slot]] * row_mask[send_slot][:, None]
        arrived = from_behind(block, "mesh", offset)
        return arrived * row_mask[recv_slot][:, None]

    def operator(field):
        gathered = field[cell_nodes]
        product = jnp.einsum("ij,cjs->cis", stiffness[0], gathered, precision=lax.Precision.HIGHEST)
        local = (
            jnp.zeros_like(field).at[cell_nodes.reshape(-1)].add(product.reshape(-1, block_cols))
        )
        from_next = trade(local, 1, 0, -grid_side)
        from_prev = trade(local, 0, 1, grid_side)
        sectioned = local.at[shared_rows[0]].add(from_next).at[shared_rows[1]].add(from_prev)
        from_right = trade(sectioned, 3, 2, -1)
        from_left = trade(sectioned, 2, 3, 1)
        assembled = sectioned.at[shared_rows[2]].add(from_right).at[shared_rows[3]].add(from_left)
        return assembled + potential[:, None] * field

    current = (operator(rotated) - center_shift * rotated) / half_width
    applied = operator(current)
    following = 2.0 * (applied - center_shift * current) / half_width - rotated
    return following


def up(size, unit):
    return -(-size // unit) * unit


def dot(left, right):
    return jnp.dot(left, right, preferred_element_type=f32)


def split(value):
    high = value.astype(bf16)
    return high, (value - high.astype(f32)).astype(bf16)


def dot3(lh, ll, rh, rl):
    return dot(lh, rh) + (dot(lh, rl) + dot(ll, rh))


def one_hot(left, right):
    return jnp.where(left == right, 1.0, 0.0).astype(bf16)


def kernel(
    nodes, face, x_ref, rot_ref, k_ref, pot_ref, ccol_ref, crow_ref, ecol_ref, erow_ref, out_ref,
    g, rbuf, c1, kh, kl, uh, ul, bh, bl, fh, fl, bv, vh, vl, rh, rl,
    half_put_a, half_got_a, half_put_b, half_got_b, put_a, got_a, put_b, got_b,
    g_send, g_recv, e_send, e_recv, r_sem,
):
    n_pad, cols = c1.shape
    half = cols // 2
    n_send = up(nodes, 8)
    mid = n_pad // 2
    tile = n_pad // 4
    cells, k_rows = ccol_ref.shape[0], k_ref.shape[0]
    me = lax.axis_index("state")
    part = lax.axis_index("mesh")

    def flip(index, bit):
        return index + bit * (1 - 2 * (index // bit % 2))

    sib, xs, ys = flip(me, 1), flip(me, 2), flip(me, 4)
    ds = flip(xs, 4)
    pair_a, pair_b = flip(part, 2), flip(part, 1)
    top, low = pl.ds(0, mid), pl.ds(mid, n_send - mid)
    whole = pl.ds(0, n_send)

    barrier = pltpu.get_barrier_semaphore()
    for target in ({"state": sib}, {"state": xs}, {"state": ys}, {"mesh": pair_a}, {"mesh": pair_b}):
        pl.semaphore_signal(barrier, inc=1, device_id=target, device_id_type=MESH)

    def load_rotation(phase):
        copies = []
        for block in range(rbuf.shape[0]):
            copy = pltpu.make_async_copy(
                rot_ref.at[pl.ds(block * cols + phase * half, half)], rbuf.at[block], r_sem.at[block]
            )
            copy.start()
            copies.append(copy)
        return copies

    rotation_copies = load_rotation(0)
    last = n_pad - 32 if nodes >= n_pad - 32 else nodes // 8 * 8
    for phase in range(2):
        g[phase, me, pl.ds(last, n_pad - last), :] = jnp.zeros((n_pad - last, half), f32)
        g[phase, me, pl.ds(0, nodes), :] = x_ref[:, phase * half : (phase + 1) * half]
    pl.semaphore_wait(barrier, 5)

    def send(phase, number, owner, rows, target):
        return pltpu.make_async_remote_copy(
            src_ref=g.at[phase, owner, rows],
            dst_ref=g.at[phase, owner, rows],
            send_sem=g_send.at[phase, number],
            recv_sem=g_recv.at[phase, number],
            device_id={"state": target},
            device_id_type=MESH,
        )

    def plan(phase):
        return [
            send(phase, 0, me, top, xs),
            send(phase, 1, me, low, xs),
            send(phase, 2, ys, low, xs),
            send(phase, 3, me, low, ys),
            send(phase, 4, me, top, ys),
            send(phase, 5, xs, top, ys),
            send(phase, 6, me, whole, sib),
            send(phase, 7, xs, top, sib),
            send(phase, 8, xs, low, sib),
            send(phase, 9, ys, low, sib),
            send(phase, 10, ys, top, sib),
            send(phase, 11, ds, low, sib),
            send(phase, 12, ds, top, sib),
        ]

    plans = [plan(0), plan(1)]

    def begin(phase):
        for number in (0, 3, 6, 1, 4):
            plans[phase][number].start()

    def pass_first(phase):
        moves = plans[phase]
        moves[3].wait_recv()
        moves[2].start()
        moves[9].start()
        moves[0].wait_recv()
        moves[5].start()
        moves[7].start()

    def pass_second(phase):
        moves = plans[phase]
        moves[1].wait_recv()
        moves[8].start()
        moves[4].wait_recv()
        moves[10].start()

    def pass_third(phase):
        moves = plans[phase]
        moves[2].wait_recv()
        moves[11].start()
        moves[5].wait_recv()
        moves[12].start()

    def arrived(phase, *numbers):
        for number in numbers:
            plans[phase][number].wait_recv()

    begin(0)

    kh[...], kl[...] = split(k_ref[...])

    def build(start, width):
        here = pl.ds(start, width)
        ids = lax.broadcasted_iota(jnp.int32, (k_ref.shape[1], width), 1) + start
        for cell in range(cells):
            pick = one_hot(ccol_ref[cell], ids)
            rows = pl.ds(cell * k_rows, k_rows)
            uh[rows, 0:width] = dot(kh[...], pick).astype(bf16)
            ul[rows, 0:width] = dot(kl[...], pick).astype(bf16)
        ends = ecol_ref[...]
        pick = jnp.where((ends == crow_ref[...]) & (ends >= 0), 1.0, 0.0).astype(bf16)
        sent = (dot(pick, uh[:, 0:width]) + dot(pick, ul[:, 0:width])) * (1.0 / half_width)
        fh[:, here], fl[:, here] = split(sent)

        def rows_step(step, carry):
            first = pl.multiple_of(step * tile, 32)
            ids = lax.broadcasted_iota(jnp.int32, (tile, crow_ref.shape[1]), 0) + first
            place = one_hot(ids, crow_ref[...])
            value = dot(place, uh[:, 0:width]) + dot(place, ul[:, 0:width])
            row = lax.broadcasted_iota(jnp.int32, (tile, width), 0) + first
            col = lax.broadcasted_iota(jnp.int32, (tile, width), 1) + start
            value = value + jnp.where(row == col, pot_ref[:, here] - center_shift, 0.0)
            high, rest = split(value * (1.0 / half_width))
            bh[pl.ds(first, tile), here] = high
            bl[pl.ds(first, tile), here] = rest
            return carry

        lax.fori_loop(0, n_pad // tile, rows_step, 0)

    wide = 256
    lax.fori_loop(
        0, n_pad // wide, lambda step, carry: (build(pl.multiple_of(step * wide, wide), wide), carry)[1], 0
    )
    if n_pad % wide:
        build(n_pad // wide * wide, n_pad % wide)

    def row_tiles(body):
        def step(index, carry):
            body(pl.ds(pl.multiple_of(index * tile, 32), tile))
            return carry

        lax.fori_loop(0, n_pad // tile, step, 0)

    def rotate(phase, owner, total, fresh=False):
        rh[...], rl[...] = split(rbuf[owner])

        def body(rows):
            high, rest = split(g[phase, owner, rows, :])
            value = dot3(high, rest, rh[...], rl[...])
            total[rows, :] = value if fresh else total[rows, :] + value

        row_tiles(body)

    def trade(number, put, got, pair, slot):
        return pltpu.make_async_remote_copy(
            src_ref=put.at[slot],
            dst_ref=got.at[slot],
            send_sem=e_send.at[number],
            recv_sem=e_recv.at[number],
            device_id={"mesh": pair},
            device_id_type=MESH,
        )

    trades = []

    def apply(number, read, width, put_one, got_one, put_two, got_two, slot, filler, write):
        span = pl.ds(0, width)

        def part_body(rows):
            vh[rows, span], vl[rows, span] = split(read(rows))

        row_tiles(part_body)
        ends = dot3(fh[...], fl[...], vh[:, span], vl[:, span])
        put_one[slot] = ends[0:face]
        put_two[slot] = ends[face:]
        first = trade(2 * number, put_one, got_one, pair_a, slot)
        first.start()

        def main_body(rows):
            bv[rows, span] = dot3(bh[rows, :], bl[rows, :], vh[:, span], vl[:, span])

        row_tiles(main_body)
        first.wait_recv()
        one_high, one_rest = split(got_one[slot])
        long_ids = ecol_ref[face:, :]
        link = jnp.where((long_ids == erow_ref[:, 0:face]) & (long_ids >= 0), 1.0, 0.0).astype(bf16)
        put_two[slot] = put_two[slot] + (dot(link, one_high) + dot(link, one_rest))
        second = trade(2 * number + 1, put_two, got_two, pair_b, slot)
        second.start()
        filler()
        second.wait_recv()
        two_high, two_rest = split(got_two[slot])

        def last_body(rows):
            ids = lax.broadcasted_iota(jnp.int32, (tile, erow_ref.shape[1]), 0) + rows.start
            place = one_hot(ids, erow_ref[...])
            near, far = place[:, 0:face], place[:, face:]
            value = dot(near, one_high) + dot(near, one_rest) + dot(far, two_high) + dot(far, two_rest)
            write(rows, bv[rows, span] + value)

        row_tiles(last_body)
        trades.extend((first, second))

    pass_first(0)
    half_span = pl.ds(0, half)

    def to_bv(width):
        def write(rows, value):
            bv[rows, pl.ds(0, width)] = value

        return write

    def filler_one():
        for copy in rotation_copies:
            copy.wait()
        rotate(0, me, c1, fresh=True)
        arrived(0, 6)
        rotate(0, sib, c1)

    def filler_two():
        pass_second(0)
        rotate(0, xs, c1)

    def finish_half(rows, value):
        g[1, me, rows, :] = 2.0 * value - g[1, me, rows, :]

    half_buffers = (half_put_a, half_got_a, half_put_b, half_got_b)
    buffers = (put_a, got_a, put_b, got_b)
    apply(0, lambda rows: g[1, me, rows, :], half, *half_buffers, 0, filler_one, to_bv(half))
    apply(1, lambda rows: bv[rows, half_span], half, *half_buffers, 1, filler_two, finish_half)
    begin(1)
    rotate(0, ys, c1)
    arrived(0, 7, 8)
    rotate(0, flip(xs, 1), c1)
    arrived(0, 9, 10)
    rotate(0, flip(ys, 1), c1)
    pass_third(0)
    rotate(0, ds, c1)
    arrived(0, 11, 12)
    rotate(0, flip(ds, 1), c1)
    rotation_copies = load_rotation(1)
    c1[pl.ds(n_send, n_pad - n_send), :] = jnp.zeros((n_pad - n_send, cols), f32)

    def filler_three():
        for copy in rotation_copies:
            copy.wait()
        rotate(1, me, out_ref, fresh=True)

    def filler_four():
        arrived(1, 6)
        rotate(1, sib, out_ref)

    def finish_whole(rows, value):
        out_ref[rows, :] = out_ref[rows, :] + (2.0 * value - c1[rows, :])

    apply(2, lambda rows: c1[rows, :], cols, *buffers, 0, filler_three, to_bv(cols))
    pass_first(1)
    apply(3, lambda rows: bv[rows, :], cols, *buffers, 1, filler_four, finish_whole)
    pass_second(1)
    rotate(1, xs, out_ref)
    rotate(1, ys, out_ref)
    arrived(1, 7, 8)
    rotate(1, flip(xs, 1), out_ref)
    arrived(1, 9, 10)
    rotate(1, flip(ys, 1), out_ref)
    pass_third(1)
    rotate(1, ds, out_ref)
    arrived(1, 11, 12)
    rotate(1, flip(ds, 1), out_ref)
    for moves in plans:
        for move in moves:
            move.wait_send()
    for move in trades:
        move.wait_send()


def square_device(states_in, rotation, stiffness, potential, cell_nodes, shared_rows, shared_count):
    nodes, cols = states_in.shape
    half = cols // 2
    blocks = lax.axis_size("state")
    n_pad = up(nodes, 128)
    npc = stiffness.shape[1]
    cells = cell_nodes.shape[0]
    k_rows, k_cols = up(npc, 32), up(npc, 128)
    side = round(npc ** (1 / 3))
    face_nodes, share = side * side, shared_rows.shape[1]
    face, long = up(face_nodes, 32), up(share, 32)
    part = lax.axis_index("mesh")
    grid_side = math.isqrt(lax.axis_size("mesh"))

    used = jnp.where(
        jnp.arange(share)[None, :] < shared_count[0][:, None], shared_rows, -1
    )
    near = lax.dynamic_index_in_dim(used, part // grid_side, 0, keepdims=False)[:face_nodes]
    far = lax.dynamic_index_in_dim(used, 2 + part % grid_side, 0, keepdims=False)
    ends = jnp.concatenate(
        [
            jnp.pad(near, (0, face - face_nodes), constant_values=-1),
            jnp.pad(far, (0, long - share), constant_values=-1),
        ]
    )
    cell_col = jnp.pad(cell_nodes, ((0, 0), (0, k_cols - npc)), constant_values=-1)[:, :, None]
    cell_row = jnp.pad(cell_nodes, ((0, 0), (0, k_rows - npc)), constant_values=-1).reshape(1, -1)
    matrix = jnp.pad(stiffness[0], ((0, k_rows - npc), (0, k_cols - npc)))
    pot = jnp.pad(potential, (0, n_pad - nodes))[None, :]
    vmem = pl.BlockSpec(memory_space=pltpu.VMEM)
    scratch = [
        pltpu.VMEM((2, blocks, n_pad, half), f32),
        pltpu.VMEM((blocks, half, cols), f32),
        pltpu.VMEM((n_pad, cols), f32),
        pltpu.VMEM((k_rows, k_cols), bf16),
        pltpu.VMEM((k_rows, k_cols), bf16),
        pltpu.VMEM((cells * k_rows, 256), bf16),
        pltpu.VMEM((cells * k_rows, 256), bf16),
        pltpu.VMEM((n_pad, n_pad), bf16),
        pltpu.VMEM((n_pad, n_pad), bf16),
        pltpu.VMEM((face + long, n_pad), bf16),
        pltpu.VMEM((face + long, n_pad), bf16),
        pltpu.VMEM((n_pad, cols), f32),
        pltpu.VMEM((n_pad, cols), bf16),
        pltpu.VMEM((n_pad, cols), bf16),
        pltpu.VMEM((half, cols), bf16),
        pltpu.VMEM((half, cols), bf16),
    ]
    for width in (half, cols):
        for rows in (face, face, long, long):
            scratch.append(pltpu.VMEM((2, rows, width), f32))
    scratch += [
        pltpu.SemaphoreType.DMA((2, 13)),
        pltpu.SemaphoreType.DMA((2, 13)),
        pltpu.SemaphoreType.DMA((8,)),
        pltpu.SemaphoreType.DMA((8,)),
        pltpu.SemaphoreType.DMA((blocks,)),
    ]
    padded = pl.pallas_call(
        functools.partial(kernel, nodes, face),
        out_shape=jax.ShapeDtypeStruct((n_pad, cols), f32),
        in_specs=[vmem, pl.BlockSpec(memory_space=pl.ANY)] + [vmem] * 6,
        out_specs=vmem,
        scratch_shapes=scratch,
        compiler_params=pltpu.CompilerParams(
            collective_id=0, has_side_effects=True, vmem_limit_bytes=64 * 1024 * 1024
        ),
    )(states_in, rotation, matrix, pot, cell_col, cell_row, ends[:, None], ends[None, :])
    return padded[:nodes]


def solution(mesh):
    squares = mesh.shape["state"] == 2 * 2 * 2 and mesh.shape["mesh"] == 2 * 2
    return jax.shard_map(
        square_device if squares else per_device,
        mesh=mesh,
        in_specs=(
            P("mesh", "state"),
            P(None, "state"),
            P("mesh", None, None),
            P("mesh"),
            P("mesh", None),
            P("mesh", None),
            P("mesh", None),
        ),
        out_specs=P("mesh", "state"),
        check_vma=False,
    )
```

```python
import functools
import math

import jax
import jax.numpy as jnp
from jax import lax
from jax.experimental import pallas as pl
from jax.experimental.pallas import tpu as pltpu
from jax.sharding import PartitionSpec as P

center_shift = 3.0
half_width = 4.0
f32 = jnp.float32
bf16 = jnp.bfloat16
MESH = pl.DeviceIdType.MESH


def from_behind(value, axis, steps):
    count = lax.axis_size(axis)
    first, last = (max(0, -steps), min(count, count - steps))
    return lax.ppermute(value, axis, [(source, source + steps) for source in range(first, last)])


def matmul(left, right):
    return jnp.dot(left, right, precision=lax.Precision.HIGHEST, preferred_element_type=jnp.float32)


def per_device(states_in, rotation, stiffness, potential, cell_nodes, shared_rows, shared_count):
    block_cols = states_in.shape[1]
    rotated = matmul(lax.all_gather(states_in, "state", axis=1, tiled=True), rotation)
    grid_side = math.isqrt(lax.axis_size("mesh"))
    row_mask = (jnp.arange(shared_rows.shape[1])[None, :] < shared_count[0][:, None]).astype(
        jnp.float32
    )

    def trade(values, send_slot, recv_slot, offset):
        block = values[shared_rows[send_slot]] * row_mask[send_slot][:, None]
        arrived = from_behind(block, "mesh", offset)
        return arrived * row_mask[recv_slot][:, None]

    def operator(field):
        gathered = field[cell_nodes]
        product = jnp.einsum("ij,cjs->cis", stiffness[0], gathered, precision=lax.Precision.HIGHEST)
        local = (
            jnp.zeros_like(field).at[cell_nodes.reshape(-1)].add(product.reshape(-1, block_cols))
        )
        from_next = trade(local, 1, 0, -grid_side)
        from_prev = trade(local, 0, 1, grid_side)
        sectioned = local.at[shared_rows[0]].add(from_next).at[shared_rows[1]].add(from_prev)
        from_right = trade(sectioned, 3, 2, -1)
        from_left = trade(sectioned, 2, 3, 1)
        assembled = sectioned.at[shared_rows[2]].add(from_right).at[shared_rows[3]].add(from_left)
        return assembled + potential[:, None] * field

    current = (operator(rotated) - center_shift * rotated) / half_width
    applied = operator(current)
    following = 2.0 * (applied - center_shift * current) / half_width - rotated
    return following


def up(size, unit):
    return -(-size // unit) * unit


def dot(left, right):
    return jnp.dot(left, right, preferred_element_type=f32)


def split(value):
    high = value.astype(bf16)
    return high, (value - high.astype(f32)).astype(bf16)


def dot3(lh, ll, rh, rl):
    return dot(lh, rh) + (dot(lh, rl) + dot(ll, rh))


def dot2(left, rh, rl):
    return dot(left, rh) + dot(left, rl)


def one_hot(left, right):
    return jnp.where(left == right, 1.0, 0.0).astype(bf16)


def one_hot_used(left, right):
    return jnp.where((left == right) & (left >= 0), 1.0, 0.0).astype(bf16)


def to_column(row):
    spread = jnp.broadcast_to(row.astype(f32), (128, row.shape[1]))
    return jnp.transpose(spread)[:, 0:1].astype(jnp.int32)


def kernel(
    grid_side, near_rows, far_rows,
    x_ref, rot_ref, k_ref, pot_ref, cells_ref, lists_ref, count_ref, out_ref,
    g, rbuf, c1, kh, kl, pick, same, gh, gl, ph, pl_, bv, rh, rl,
    pot, crow, crep, ccol, dcol, near_row, far_row, near_col, far_col,
    put_a, got_a, put_b, got_b,
    g_send, g_recv, e_send, e_recv, r_sem,
):
    nodes = x_ref.shape[0]
    n_pad, cols = c1.shape
    half = cols // 2
    n_send = up(nodes, 8)
    mid = n_pad // 2
    tile = n_pad // 4
    cells, npc = cells_ref.shape
    stride = kh.shape[0]
    side = 256
    me = lax.axis_index("state")
    part = lax.axis_index("mesh")

    def flip(index, bit):
        return index + bit * (1 - 2 * (index // bit % 2))

    sib, xs, ys = flip(me, 1), flip(me, 2), flip(me, 4)
    ds = flip(xs, 4)
    pair_a, pair_b = flip(part, grid_side), flip(part, 1)
    top, low = pl.ds(0, mid), pl.ds(mid, n_send - mid)
    whole = pl.ds(0, n_send)

    barrier = pltpu.get_barrier_semaphore()
    for target in ({"state": sib}, {"state": xs}, {"state": ys}, {"mesh": pair_a}, {"mesh": pair_b}):
        pl.semaphore_signal(barrier, inc=1, device_id=target, device_id_type=MESH)

    def load_rotation(phase):
        copies = []
        for block in range(rbuf.shape[0]):
            copy = pltpu.make_async_copy(
                rot_ref.at[pl.ds(block * cols + phase * half, half)], rbuf.at[block], r_sem.at[block]
            )
            copy.start()
            copies.append(copy)
        return copies

    rotation_copies = load_rotation(0)
    last = nodes // 8 * 8
    for phase in range(2):
        g[phase, me, pl.ds(last, n_pad - last), :] = jnp.zeros((n_pad - last, half), f32)
        g[phase, me, pl.ds(0, nodes), :] = x_ref[:, phase * half : (phase + 1) * half]
    pl.semaphore_wait(barrier, 5)

    def send(phase, number, owner, rows, target):
        return pltpu.make_async_remote_copy(
            src_ref=g.at[phase, owner, rows],
            dst_ref=g.at[phase, owner, rows],
            send_sem=g_send.at[phase, number],
            recv_sem=g_recv.at[phase, number],
            device_id={"state": target},
            device_id_type=MESH,
        )

    def plan(phase):
        return [
            send(phase, 0, me, top, xs),
            send(phase, 1, me, low, xs),
            send(phase, 2, ys, low, xs),
            send(phase, 3, me, low, ys),
            send(phase, 4, me, top, ys),
            send(phase, 5, xs, top, ys),
            send(phase, 6, me, whole, sib),
            send(phase, 7, xs, top, sib),
            send(phase, 8, xs, low, sib),
            send(phase, 9, ys, low, sib),
            send(phase, 10, ys, top, sib),
            send(phase, 11, ds, low, sib),
            send(phase, 12, ds, top, sib),
        ]

    plans = [plan(0), plan(1)]

    def begin(phase, *numbers):
        for number in numbers:
            plans[phase][number].start()

    def pass_on(phase, number, *onward):
        plans[phase][number].wait_recv()
        begin(phase, *onward)

    def pass_first(phase):
        pass_on(phase, 3, 2, 9)
        pass_on(phase, 0, 5, 7)

    def pass_second(phase):
        pass_on(phase, 1, 8)
        pass_on(phase, 4, 10)

    def pass_third(phase):
        pass_on(phase, 2, 11)
        pass_on(phase, 5, 12)

    def arrived(phase, *numbers):
        for number in numbers:
            plans[phase][number].wait_recv()

    begin(0, 0, 3, 6)

    def tiles(count, size, body):
        def step(index, carry):
            body(pl.ds(pl.multiple_of(index * size, 32), size))
            return carry

        lax.fori_loop(0, count // size, step, 0)

    pot[...] = jnp.zeros(pot.shape, f32)
    pot[:, 0:nodes] = pot_ref[...]
    crow[...] = jnp.full(crow.shape, -1, jnp.int32)
    for cell in range(cells):
        crow[:, cell * stride : cell * stride + npc] = cells_ref[cell : cell + 1, :]
    near_row[...] = jnp.full(near_row.shape, -1, jnp.int32)
    far_row[...] = jnp.full(far_row.shape, -1, jnp.int32)
    for row_ref, offset, place in ((near_row, 0, part // grid_side), (far_row, 2, part % grid_side)):
        size = near_rows if row_ref is near_row else far_rows
        ids = lax.broadcasted_iota(jnp.int32, (1, size), 1)
        second = place == 1
        listed = jnp.where(
            second, lists_ref[offset + 1 : offset + 2, 0:size], lists_ref[offset : offset + 1, 0:size]
        )
        count = jnp.where(second, count_ref[0, offset + 1], count_ref[0, offset])
        row_ref[:, 0:size] = jnp.where(ids < count, listed, -1)
    near_col[...] = to_column(near_row[...])[0 : near_col.shape[0]]
    far_col[...] = to_column(far_row[...])[0 : far_col.shape[0]]
    ccol[...] = to_column(crow[...])

    for first in range(0, stride, cols):
        width = min(cols, stride - first)
        used = min(npc - first, width)
        out_ref[0:stride, 0:width] = jnp.zeros((stride, width), f32)
        out_ref[0:npc, 0:used] = k_ref[0, :, first : first + used]
        span = slice(first, first + width)
        kh[:, span], kl[:, span] = split(out_ref[0:stride, 0:width])

    def pick_body(rows):
        ids = lax.broadcasted_iota(jnp.int32, (side, n_pad), 1)
        here = ccol[rows, :] == ids
        pick[rows, :] = jnp.where(here, 1.0, 0.0).astype(bf16)
        dcol[rows, :] = jnp.sum(jnp.where(here, pot[...], 0.0), axis=1, keepdims=True) - center_shift

    tiles(cells * stride, side, pick_body)
    crep[...] = crow[...]
    pairs = [(one, two) for one in range(cells) for two in range(cells) if one != two]
    for index, (one, two) in enumerate(pairs):
        left = ccol[one * stride : (one + 1) * stride, :]
        span = slice(two * stride, (two + 1) * stride)
        both = one_hot_used(left, crow[:, span])
        same[index] = both
        if one < two:
            taken = jnp.max(both.astype(f32), axis=0, keepdims=True)
            crep[:, span] = jnp.where(taken > 0.5, -1, crep[:, span])

    begin(0, 1, 4)

    def rotate(phase, owner, total, fresh=False):
        rh[...], rl[...] = split(rbuf[owner])

        def body(rows):
            high, rest = split(g[phase, owner, rows, :])
            value = dot3(high, rest, rh[...], rl[...])
            total[rows, :] = value if fresh else total[rows, :] + value

        tiles(n_pad, tile, body)

    def trade(field, number, which):
        put, got, pair = ((put_a, got_a, pair_a), (put_b, got_b, pair_b))[which]
        slot = 2 * field + number
        return pltpu.make_async_remote_copy(
            src_ref=put.at[slot],
            dst_ref=got.at[slot],
            send_sem=e_send.at[which, slot],
            recv_sem=e_recv.at[which, slot],
            device_id={"mesh": pair},
            device_id_type=MESH,
        )

    def enter(bank, read):
        def split_body(rows):
            ph[bank, rows, :], pl_[bank, rows, :] = split(read(rows))

        tiles(n_pad, tile, split_body)

        def body(rows):
            gh[bank, rows, :] = dot(pick[rows, :], ph[bank, 0:n_pad, :]).astype(bf16)
            gl[bank, rows, :] = dot(pick[rows, :], pl_[bank, 0:n_pad, :]).astype(bf16)

        tiles(cells * stride, side, body)

    def product(bank, field, number):
        for cell in range(cells):
            span = slice(cell * stride, (cell + 1) * stride)

            def body(rows):
                value = dot3(kh[rows, :], kl[rows, :], gh[bank, span, :], gl[bank, span, :])
                here = pl.ds(pl.multiple_of(rows.start + cell * stride, 32), side)
                ph[bank, here, :], pl_[bank, here, :] = split(value)
                held = gh[bank, here, :].astype(f32) + gl[bank, here, :].astype(f32)
                bv[bank, here, :] = value + dcol[here, :] * held

            tiles(stride, side, body)
        slot = 2 * field + number
        for put, col in ((put_a, near_col), (put_b, far_col)):
            put[slot] = dot2(one_hot_used(col[...], crow[...]), ph[bank], pl_[bank])
            if put is put_a:
                trade(field, number, 0).start()

    def couple(bank):
        for index, (one, two) in enumerate(pairs):
            span = slice(two * stride, (two + 1) * stride)

            def body(rows):
                here = pl.ds(pl.multiple_of(rows.start + one * stride, 32), side)
                value = dot2(same[index, rows, :], ph[bank, span, :], pl_[bank, span, :])
                bv[bank, here, :] = bv[bank, here, :] + value

            tiles(stride, side, body)

    def link(field, number):
        slot = 2 * field + number
        trade(field, number, 0).wait_recv()
        corner = one_hot_used(far_col[...], near_row[:, 0 : near_col.shape[0]])
        put_b[slot] = put_b[slot] + dot2(corner, *split(got_a[slot]))
        trade(field, number, 1).start()

    def finish(bank, field, number):
        slot = 2 * field + number
        trade(field, number, 1).wait_recv()
        near_high, near_rest = split(got_a[slot])
        far_high, far_rest = split(got_b[slot])

        def body(rows):
            near = one_hot_used(ccol[rows, :], near_row[:, 0 : near_col.shape[0]])
            far = one_hot_used(ccol[rows, :], far_row[:, 0 : far_col.shape[0]])
            value = bv[bank, rows, :] + dot2(near, near_high, near_rest)
            value = value + dot2(far, far_high, far_rest)
            gh[bank, rows, :], gl[bank, rows, :] = split(value * (1.0 / half_width))

        tiles(cells * stride, side, body)

    def leave(bank, write):
        def body(rows):
            ids = lax.broadcasted_iota(jnp.int32, (tile, crep.shape[1]), 0) + rows.start
            write(rows, dot2(one_hot(ids, crep[...]), gh[bank], gl[bank]))

        tiles(n_pad, tile, body)

    enter(0, lambda rows: g[1, me, rows, :])
    product(0, 0, 0)
    couple(0)
    for copy in rotation_copies:
        copy.wait()
    rotate(0, me, c1, fresh=True)
    link(0, 0)
    arrived(0, 6)
    rotate(0, sib, c1)
    finish(0, 0, 0)
    product(0, 0, 1)
    couple(0)
    pass_first(0)
    link(0, 1)
    finish(0, 0, 1)

    def leave_half(rows, value):
        g[1, me, rows, :] = 2.0 * value - g[1, me, rows, :]

    leave(0, leave_half)
    begin(1, 0, 3, 6)
    pass_second(0)
    rotate(0, xs, c1)
    rotate(0, ys, c1)
    arrived(0, 7, 8)
    rotate(0, flip(xs, 1), c1)
    arrived(0, 9, 10)
    rotate(0, flip(ys, 1), c1)
    pass_third(0)
    begin(1, 1, 4)
    rotate(0, ds, c1)
    arrived(0, 11, 12)
    rotate(0, flip(ds, 1), c1)
    rotation_copies = load_rotation(1)
    c1[pl.ds(n_send, n_pad - n_send), :] = jnp.zeros((n_pad - n_send, cols), f32)

    spans = [slice(0, half), slice(half, cols)]

    for bank in range(2):
        enter(bank, lambda rows: c1[rows, spans[bank]])
        product(bank, bank + 1, 0)
    for bank in range(2):
        couple(bank)
        link(bank + 1, 0)
    for copy in rotation_copies:
        copy.wait()
    rotate(1, me, out_ref, fresh=True)
    pass_first(1)
    for bank in range(2):
        finish(bank, bank + 1, 0)
        product(bank, bank + 1, 1)
    for bank in range(2):
        couple(bank)
        link(bank + 1, 1)
    arrived(1, 6)
    rotate(1, sib, out_ref)
    pass_second(1)
    for bank in range(2):
        finish(bank, bank + 1, 1)

        def leave_whole(rows, value):
            span = spans[bank]
            out_ref[rows, span] = out_ref[rows, span] + (2.0 * value - c1[rows, span])

        leave(bank, leave_whole)
    rotate(1, xs, out_ref)
    rotate(1, ys, out_ref)
    pass_third(1)
    arrived(1, 7, 8)
    rotate(1, flip(xs, 1), out_ref)
    arrived(1, 9, 10)
    rotate(1, flip(ys, 1), out_ref)
    rotate(1, ds, out_ref)
    arrived(1, 11, 12)
    rotate(1, flip(ds, 1), out_ref)
    for moves in plans:
        for move in moves:
            move.wait_send()
    for field in range(3):
        for number in range(2):
            for which in range(2):
                trade(field, number, which).wait_send()


def square_device(states_in, rotation, stiffness, potential, cell_nodes, shared_rows, shared_count):
    nodes, cols = states_in.shape
    half = cols // 2
    blocks = lax.axis_size("state")
    n_pad = up(nodes, 128)
    cells, npc = cell_nodes.shape
    stride = up(npc, 256)
    side = round(npc ** (1 / 3))
    near_rows, far_rows = side * side, shared_rows.shape[1]
    near, far = up(near_rows, 32), up(far_rows, 32)
    grid_side = math.isqrt(lax.axis_size("mesh"))
    vmem = pl.BlockSpec(memory_space=pltpu.VMEM)
    smem = pl.BlockSpec(memory_space=pltpu.SMEM)
    scratch = [
        pltpu.VMEM((2, blocks, n_pad, half), f32),
        pltpu.VMEM((blocks, half, cols), f32),
        pltpu.VMEM((n_pad, cols), f32),
        pltpu.VMEM((stride, stride), bf16),
        pltpu.VMEM((stride, stride), bf16),
        pltpu.VMEM((cells * stride, n_pad), bf16),
        pltpu.VMEM((cells * (cells - 1), stride, stride), bf16),
        pltpu.VMEM((2, cells * stride, half), bf16),
        pltpu.VMEM((2, cells * stride, half), bf16),
        pltpu.VMEM((2, cells * stride, half), bf16),
        pltpu.VMEM((2, cells * stride, half), bf16),
        pltpu.VMEM((2, cells * stride, half), f32),
        pltpu.VMEM((half, cols), bf16),
        pltpu.VMEM((half, cols), bf16),
        pltpu.VMEM((1, n_pad), f32),
        pltpu.VMEM((1, cells * stride), jnp.int32),
        pltpu.VMEM((1, cells * stride), jnp.int32),
        pltpu.VMEM((cells * stride, 1), jnp.int32),
        pltpu.VMEM((cells * stride, 1), f32),
        pltpu.VMEM((1, up(near, 128)), jnp.int32),
        pltpu.VMEM((1, up(far, 128)), jnp.int32),
        pltpu.VMEM((near, 1), jnp.int32),
        pltpu.VMEM((far, 1), jnp.int32),
        pltpu.VMEM((6, near, half), f32),
        pltpu.VMEM((6, near, half), f32),
        pltpu.VMEM((6, far, half), f32),
        pltpu.VMEM((6, far, half), f32),
        pltpu.SemaphoreType.DMA((2, 13)),
        pltpu.SemaphoreType.DMA((2, 13)),
        pltpu.SemaphoreType.DMA((2, 6)),
        pltpu.SemaphoreType.DMA((2, 6)),
        pltpu.SemaphoreType.DMA((blocks,)),
    ]
    padded = pl.pallas_call(
        functools.partial(kernel, grid_side, near_rows, far_rows),
        out_shape=jax.ShapeDtypeStruct((n_pad, cols), f32),
        in_specs=[vmem, pl.BlockSpec(memory_space=pl.ANY), vmem, vmem, vmem, vmem, smem],
        out_specs=vmem,
        scratch_shapes=scratch,
        compiler_params=pltpu.CompilerParams(
            collective_id=0, has_side_effects=True, vmem_limit_bytes=64 * 1024 * 1024
        ),
    )(
        states_in, rotation, stiffness, potential[None, :], cell_nodes, shared_rows, shared_count
    )
    return padded[:nodes]


def solution(mesh):
    squares = mesh.shape["state"] == 2 * 2 * 2 and mesh.shape["mesh"] == 2 * 2
    return jax.shard_map(
        square_device if squares else per_device,
        mesh=mesh,
        in_specs=(
            P("mesh", "state"),
            P(None, "state"),
            P("mesh", None, None),
            P("mesh"),
            P("mesh", None),
            P("mesh", None),
            P("mesh", None),
        ),
        out_specs=P("mesh", "state"),
        check_vma=False,
    )
```

```python
import functools
import math

import jax
import jax.numpy as jnp
from jax import lax
from jax.experimental import pallas as pl
from jax.experimental.pallas import tpu as pltpu
from jax.sharding import PartitionSpec as P

center_shift = 3.0
half_width = 4.0
f32 = jnp.float32
bf16 = jnp.bfloat16
MESH = pl.DeviceIdType.MESH


def from_behind(value, axis, steps):
    count = lax.axis_size(axis)
    first, last = (max(0, -steps), min(count, count - steps))
    return lax.ppermute(value, axis, [(source, source + steps) for source in range(first, last)])


def matmul(left, right):
    return jnp.dot(left, right, precision=lax.Precision.HIGHEST, preferred_element_type=jnp.float32)


def per_device(states_in, rotation, stiffness, potential, cell_nodes, shared_rows, shared_count):
    block_cols = states_in.shape[1]
    rotated = matmul(lax.all_gather(states_in, "state", axis=1, tiled=True), rotation)
    grid_side = math.isqrt(lax.axis_size("mesh"))
    row_mask = (jnp.arange(shared_rows.shape[1])[None, :] < shared_count[0][:, None]).astype(
        jnp.float32
    )

    def trade(values, send_slot, recv_slot, offset):
        block = values[shared_rows[send_slot]] * row_mask[send_slot][:, None]
        arrived = from_behind(block, "mesh", offset)
        return arrived * row_mask[recv_slot][:, None]

    def operator(field):
        gathered = field[cell_nodes]
        product = jnp.einsum("ij,cjs->cis", stiffness[0], gathered, precision=lax.Precision.HIGHEST)
        local = (
            jnp.zeros_like(field).at[cell_nodes.reshape(-1)].add(product.reshape(-1, block_cols))
        )
        from_next = trade(local, 1, 0, -grid_side)
        from_prev = trade(local, 0, 1, grid_side)
        sectioned = local.at[shared_rows[0]].add(from_next).at[shared_rows[1]].add(from_prev)
        from_right = trade(sectioned, 3, 2, -1)
        from_left = trade(sectioned, 2, 3, 1)
        assembled = sectioned.at[shared_rows[2]].add(from_right).at[shared_rows[3]].add(from_left)
        return assembled + potential[:, None] * field

    current = (operator(rotated) - center_shift * rotated) / half_width
    applied = operator(current)
    following = 2.0 * (applied - center_shift * current) / half_width - rotated
    return following


def up(size, unit):
    return -(-size // unit) * unit


def dot(left, right):
    return jnp.dot(left, right, preferred_element_type=f32)


def split(value):
    high = value.astype(bf16)
    return high, (value - high.astype(f32)).astype(bf16)


def dot3(lh, ll, rh, rl):
    return dot(lh, rh) + (dot(lh, rl) + dot(ll, rh))


def dot2(left, rh, rl):
    return dot(left, rh) + dot(left, rl)


def one_hot(left, right):
    return jnp.where(left == right, 1.0, 0.0).astype(bf16)


def one_hot_used(left, right):
    return jnp.where((left == right) & (left >= 0), 1.0, 0.0).astype(bf16)


def to_column(row):
    spread = jnp.broadcast_to(row.astype(f32), (128, row.shape[1]))
    return jnp.transpose(spread)[:, 0:1].astype(jnp.int32)


def kernel(
    grid_side, near_rows, far_rows,
    x_ref, rot_ref, k_ref, pot_ref, cells_ref, lists_ref, count_ref, out_ref,
    g, rbuf, c1, kh, kl, pick, same, gh, gl, ph, pl_, bv, r3,
    pot, crow, crep, ccol, dcol, near_row, far_row, near_col, far_col,
    half_put_a, half_got_a, half_put_b, half_got_b, put_a, got_a, put_b, got_b,
    g_send, g_recv, e_send, e_recv, r_sem,
):
    nodes = x_ref.shape[0]
    n_pad, cols = c1.shape
    half = cols // 2
    n_send = up(nodes, 8)
    mid = n_pad // 2
    tile = n_pad // 2
    cells, npc = cells_ref.shape
    stride = kh.shape[0]
    side = stride // 2
    me = lax.axis_index("state")
    part = lax.axis_index("mesh")

    def flip(index, bit):
        return index + bit * (1 - 2 * (index // bit % 2))

    sib, xs, ys = flip(me, 1), flip(me, 2), flip(me, 4)
    ds = flip(xs, 4)
    pair_a, pair_b = flip(part, grid_side), flip(part, 1)
    top, low = pl.ds(0, mid), pl.ds(mid, n_send - mid)
    whole = pl.ds(0, n_send)

    barrier = pltpu.get_barrier_semaphore()
    for target in ({"state": sib}, {"state": xs}, {"state": ys}, {"mesh": pair_a}, {"mesh": pair_b}):
        pl.semaphore_signal(barrier, inc=1, device_id=target, device_id_type=MESH)

    def load_rotation(phase):
        copies = []
        for block in range(rbuf.shape[0]):
            copy = pltpu.make_async_copy(
                rot_ref.at[pl.ds(block * cols + phase * half, half)], rbuf.at[block], r_sem.at[block]
            )
            copy.start()
            copies.append(copy)
        return copies

    rotation_copies = load_rotation(0)
    last = nodes // 8 * 8
    for phase in range(2):
        g[phase, me, pl.ds(last, n_pad - last), :] = jnp.zeros((n_pad - last, half), f32)
        g[phase, me, pl.ds(0, nodes), :] = x_ref[:, phase * half : (phase + 1) * half]
    pl.semaphore_wait(barrier, 5)

    def send(phase, number, owner, rows, target):
        return pltpu.make_async_remote_copy(
            src_ref=g.at[phase, owner, rows],
            dst_ref=g.at[phase, owner, rows],
            send_sem=g_send.at[phase, number],
            recv_sem=g_recv.at[phase, number],
            device_id={"state": target},
            device_id_type=MESH,
        )

    def plan(phase):
        return [
            send(phase, 0, me, top, xs),
            send(phase, 1, me, low, xs),
            send(phase, 2, ys, low, xs),
            send(phase, 3, me, low, ys),
            send(phase, 4, me, top, ys),
            send(phase, 5, xs, top, ys),
            send(phase, 6, me, whole, sib),
            send(phase, 7, xs, top, sib),
            send(phase, 8, xs, low, sib),
            send(phase, 9, ys, low, sib),
            send(phase, 10, ys, top, sib),
            send(phase, 11, ds, low, sib),
            send(phase, 12, ds, top, sib),
        ]

    plans = [plan(0), plan(1)]

    def begin(phase, *numbers):
        for number in numbers:
            plans[phase][number].start()

    def pass_on(phase, number, *onward):
        plans[phase][number].wait_recv()
        begin(phase, *onward)

    def pass_first(phase):
        pass_on(phase, 3, 2, 9)
        pass_on(phase, 0, 5, 7)

    def pass_second(phase):
        pass_on(phase, 1, 8)
        pass_on(phase, 4, 10)

    def pass_third(phase):
        pass_on(phase, 2, 11)
        pass_on(phase, 5, 12)

    def arrived(phase, *numbers):
        for number in numbers:
            plans[phase][number].wait_recv()

    begin(0, 0, 3, 6)

    def tiles(count, size, body):
        def step(index, carry):
            body(pl.ds(pl.multiple_of(index * size, 32), size))
            return carry

        lax.fori_loop(0, count // size, step, 0)

    pot[...] = jnp.zeros(pot.shape, f32)
    pot[:, 0:nodes] = pot_ref[...].reshape(1, nodes)
    crow[...] = jnp.full(crow.shape, -1, jnp.int32)
    for cell in range(cells):
        crow[:, cell * stride : cell * stride + npc] = cells_ref[cell : cell + 1, :]
    near_row[...] = jnp.full(near_row.shape, -1, jnp.int32)
    far_row[...] = jnp.full(far_row.shape, -1, jnp.int32)
    for row_ref, offset, place in ((near_row, 0, part // grid_side), (far_row, 2, part % grid_side)):
        size = near_rows if row_ref is near_row else far_rows
        ids = lax.broadcasted_iota(jnp.int32, (1, size), 1)
        second = place == 1
        listed = jnp.where(
            second, lists_ref[offset + 1 : offset + 2, 0:size], lists_ref[offset : offset + 1, 0:size]
        )
        count = jnp.where(second, count_ref[0, offset + 1], count_ref[0, offset])
        row_ref[:, 0:size] = jnp.where(ids < count, listed, -1)
    near_col[...] = to_column(near_row[...])[0 : near_col.shape[0]]
    far_col[...] = to_column(far_row[...])[0 : far_col.shape[0]]
    ccol[...] = to_column(crow[...])

    for first in range(0, stride, cols):
        width = min(cols, stride - first)
        used = min(npc - first, width)
        out_ref[0:stride, 0:width] = jnp.zeros((stride, width), f32)
        out_ref[0:npc, 0:used] = k_ref[0, :, first : first + used]
        span = slice(first, first + width)
        kh[:, span], kl[:, span] = split(out_ref[0:stride, 0:width])

    def pick_body(rows):
        ids = lax.broadcasted_iota(jnp.int32, (side, n_pad), 1)
        here = ccol[rows, :] == ids
        pick[rows, :] = jnp.where(here, 1.0, 0.0).astype(bf16)
        dcol[rows, :] = jnp.sum(jnp.where(here, pot[...], 0.0), axis=1, keepdims=True) - center_shift

    tiles(cells * stride, side, pick_body)
    crep[...] = crow[...]
    pairs = [(one, two) for one in range(cells) for two in range(cells) if one != two]
    for index, (one, two) in enumerate(pairs):
        left = ccol[one * stride : (one + 1) * stride, :]
        span = slice(two * stride, (two + 1) * stride)
        both = one_hot_used(left, crow[:, span])
        same[index] = both
        if one < two:
            taken = jnp.max(both.astype(f32), axis=0, keepdims=True)
            crep[:, span] = jnp.where(taken > 0.5, -1, crep[:, span])

    begin(0, 1, 4)

    def rotate(phase, owner, total, fresh=False):
        high, rest = split(rbuf[owner])
        r3[0:half], r3[half : 2 * half], r3[2 * half :] = high, rest, high

        def body(rows):
            high, rest = split(g[phase, owner, rows, :])
            value = dot(jnp.concatenate([high, high, rest], axis=1), r3[...])
            total[rows, :] = value if fresh else total[rows, :] + value

        tiles(n_pad, tile, body)

    buffers = (
        ((half_put_a, half_got_a, pair_a), (half_put_b, half_got_b, pair_b)),
        ((put_a, got_a, pair_a), (put_b, got_b, pair_b)),
    )

    def trade(field, number, which):
        put, got, pair = buffers[field][which]
        return pltpu.make_async_remote_copy(
            src_ref=put.at[number],
            dst_ref=got.at[number],
            send_sem=e_send.at[which, 2 * field + number],
            recv_sem=e_recv.at[which, 2 * field + number],
            device_id={"mesh": pair},
            device_id_type=MESH,
        )

    def hold(field, high_ref, rest_ref, rows, value):
        high, rest = split(value)
        if field:
            high_ref[rows, :], rest_ref[rows, :] = high, rest
        else:
            high_ref[rows, 0:half], high_ref[rows, half:] = high, rest

    def fold(value):
        return value[:, 0:half] + value[:, half:]

    def times(field, left, high_ref, rest_ref, rows):
        if field:
            return dot2(left, high_ref[rows, :], rest_ref[rows, :])
        return fold(dot(left, high_ref[rows, :]))

    def times_value(field, left, value):
        high, rest = split(value)
        if field:
            return dot2(left, high, rest)
        return fold(dot(left, jnp.concatenate([high, rest], axis=1)))

    def width(field):
        return slice(0, cols if field else half)

    def enter(field, read):
        def split_body(rows):
            hold(field, ph, pl_, rows, read(rows))

        tiles(n_pad, tile, split_body)

        def body(rows):
            gh[rows, :] = dot(pick[rows, :], ph[0:n_pad, :]).astype(bf16)
            if field:
                gl[rows, :] = dot(pick[rows, :], pl_[0:n_pad, :]).astype(bf16)

        tiles(cells * stride, side, body)

    def product(field, number):
        for cell in range(cells):
            span = slice(cell * stride, (cell + 1) * stride)

            def body(rows):
                here = pl.ds(pl.multiple_of(rows.start + cell * stride, 32), side)
                value = times(field, kh[rows, :], gh, gl, span)
                value = value + dot(kl[rows, :], gh[span, width(field)])
                hold(field, ph, pl_, here, value)
                if field:
                    held = gh[here, :].astype(f32) + gl[here, :].astype(f32)
                else:
                    held = fold(gh[here, :].astype(f32))
                bv[here, width(field)] = value + dcol[here, :] * held

            tiles(stride, side, body)
        every = slice(0, cells * stride)
        for which, col in ((0, near_col), (1, far_col)):
            picked = times(field, one_hot_used(col[...], crow[...]), ph, pl_, every)
            buffers[field][which][0][number] = picked
            if which == 0:
                trade(field, number, 0).start()

    def couple(field):
        for index, (one, two) in enumerate(pairs):
            span = slice(two * stride, (two + 1) * stride)

            def body(rows):
                here = pl.ds(pl.multiple_of(rows.start + one * stride, 32), side)
                value = times(field, same[index, rows, :], ph, pl_, span)
                bv[here, width(field)] = bv[here, width(field)] + value

            tiles(stride, side, body)

    def link(field, number):
        trade(field, number, 0).wait_recv()
        corner = one_hot_used(far_col[...], near_row[:, 0 : near_col.shape[0]])
        got, put = buffers[field][0][1], buffers[field][1][0]
        put[number] = put[number] + times_value(field, corner, got[number])
        trade(field, number, 1).start()

    def finish(field, number):
        trade(field, number, 1).wait_recv()
        near_got, far_got = buffers[field][0][1], buffers[field][1][1]

        def body(rows):
            near = one_hot_used(ccol[rows, :], near_row[:, 0 : near_col.shape[0]])
            far = one_hot_used(ccol[rows, :], far_row[:, 0 : far_col.shape[0]])
            value = bv[rows, width(field)] + times_value(field, near, near_got[number])
            value = value + times_value(field, far, far_got[number])
            hold(field, gh, gl, rows, value * (1.0 / half_width))

        tiles(cells * stride, side, body)

    def leave(field, write):
        size = tile // 2

        def body(rows):
            ids = lax.broadcasted_iota(jnp.int32, (size, crep.shape[1]), 0) + rows.start
            write(rows, times(field, one_hot(ids, crep[...]), gh, gl, slice(0, cells * stride)))

        tiles(n_pad, size, body)

    enter(0, lambda rows: g[1, me, rows, :])
    product(0, 0)
    couple(0)
    for copy in rotation_copies:
        copy.wait()
    rotate(0, me, c1, fresh=True)
    link(0, 0)
    arrived(0, 6)
    rotate(0, sib, c1)
    finish(0, 0)
    product(0, 1)
    couple(0)
    pass_first(0)
    link(0, 1)
    pass_second(0)
    rotate(0, xs, c1)
    finish(0, 1)

    def leave_half(rows, value):
        g[1, me, rows, :] = 2.0 * value - g[1, me, rows, :]

    leave(0, leave_half)
    begin(1, 0, 3, 6)
    rotate(0, ys, c1)
    arrived(0, 7, 8)
    rotate(0, flip(xs, 1), c1)
    arrived(0, 9, 10)
    rotate(0, flip(ys, 1), c1)
    pass_third(0)
    begin(1, 1, 4)
    rotate(0, ds, c1)
    arrived(0, 11, 12)
    rotate(0, flip(ds, 1), c1)
    rotation_copies = load_rotation(1)
    c1[pl.ds(n_send, n_pad - n_send), :] = jnp.zeros((n_pad - n_send, cols), f32)

    enter(1, lambda rows: c1[rows, :])
    product(1, 0)
    couple(1)
    for copy in rotation_copies:
        copy.wait()
    rotate(1, me, out_ref, fresh=True)
    link(1, 0)
    pass_first(1)
    arrived(1, 6)
    rotate(1, sib, out_ref)
    finish(1, 0)
    product(1, 1)
    couple(1)
    link(1, 1)
    pass_second(1)
    rotate(1, xs, out_ref)
    rotate(1, ys, out_ref)
    finish(1, 1)

    def leave_whole(rows, value):
        out_ref[rows, :] = out_ref[rows, :] + (2.0 * value - c1[rows, :])

    leave(1, leave_whole)
    pass_third(1)
    arrived(1, 7, 8)
    rotate(1, flip(xs, 1), out_ref)
    arrived(1, 9, 10)
    rotate(1, flip(ys, 1), out_ref)
    rotate(1, ds, out_ref)
    arrived(1, 11, 12)
    rotate(1, flip(ds, 1), out_ref)
    for moves in plans:
        for move in moves:
            move.wait_send()
    for field in range(2):
        for number in range(2):
            for which in range(2):
                trade(field, number, which).wait_send()


def square_device(states_in, rotation, stiffness, potential, cell_nodes, shared_rows, shared_count):
    nodes, cols = states_in.shape
    half = cols // 2
    blocks = lax.axis_size("state")
    n_pad = up(nodes, 128)
    cells, npc = cell_nodes.shape
    stride = up(npc, 256)
    side = round(npc ** (1 / 3))
    near_rows, far_rows = side * side, shared_rows.shape[1]
    near, far = up(near_rows, 32), up(far_rows, 32)
    grid_side = math.isqrt(lax.axis_size("mesh"))
    vmem = pl.BlockSpec(memory_space=pltpu.VMEM)
    smem = pl.BlockSpec(memory_space=pltpu.SMEM)
    scratch = [
        pltpu.VMEM((2, blocks, n_pad, half), f32),
        pltpu.VMEM((blocks, half, cols), f32),
        pltpu.VMEM((n_pad, cols), f32),
        pltpu.VMEM((stride, stride), bf16),
        pltpu.VMEM((stride, stride), bf16),
        pltpu.VMEM((cells * stride, n_pad), bf16),
        pltpu.VMEM((cells * (cells - 1), stride, stride), bf16),
        pltpu.VMEM((cells * stride, cols), bf16),
        pltpu.VMEM((cells * stride, cols), bf16),
        pltpu.VMEM((cells * stride, cols), bf16),
        pltpu.VMEM((cells * stride, cols), bf16),
        pltpu.VMEM((cells * stride, cols), f32),
        pltpu.VMEM((3 * half, cols), bf16),
        pltpu.VMEM((1, n_pad), f32),
        pltpu.VMEM((1, cells * stride), jnp.int32),
        pltpu.VMEM((1, cells * stride), jnp.int32),
        pltpu.VMEM((cells * stride, 1), jnp.int32),
        pltpu.VMEM((cells * stride, 1), f32),
        pltpu.VMEM((1, up(near, 128)), jnp.int32),
        pltpu.VMEM((1, up(far, 128)), jnp.int32),
        pltpu.VMEM((near, 1), jnp.int32),
        pltpu.VMEM((far, 1), jnp.int32),
        pltpu.VMEM((2, near, half), f32),
        pltpu.VMEM((2, near, half), f32),
        pltpu.VMEM((2, far, half), f32),
        pltpu.VMEM((2, far, half), f32),
        pltpu.VMEM((2, near, cols), f32),
        pltpu.VMEM((2, near, cols), f32),
        pltpu.VMEM((2, far, cols), f32),
        pltpu.VMEM((2, far, cols), f32),
        pltpu.SemaphoreType.DMA((2, 13)),
        pltpu.SemaphoreType.DMA((2, 13)),
        pltpu.SemaphoreType.DMA((2, 4)),
        pltpu.SemaphoreType.DMA((2, 4)),
        pltpu.SemaphoreType.DMA((blocks,)),
    ]
    padded = pl.pallas_call(
        functools.partial(kernel, grid_side, near_rows, far_rows),
        out_shape=jax.ShapeDtypeStruct((n_pad, cols), f32),
        in_specs=[vmem, pl.BlockSpec(memory_space=pl.ANY), vmem, vmem, vmem, vmem, smem],
        out_specs=vmem,
        scratch_shapes=scratch,
        compiler_params=pltpu.CompilerParams(
            collective_id=0, has_side_effects=True, vmem_limit_bytes=64 * 1024 * 1024
        ),
    )(
        states_in, rotation, stiffness, potential, cell_nodes, shared_rows, shared_count
    )
    return padded[:nodes]


def solution(mesh):
    squares = mesh.shape["state"] == 2 * 2 * 2 and mesh.shape["mesh"] == 2 * 2
    return jax.shard_map(
        square_device if squares else per_device,
        mesh=mesh,
        in_specs=(
            P("mesh", "state"),
            P(None, "state"),
            P("mesh", None, None),
            P("mesh"),
            P("mesh", None),
            P("mesh", None),
            P("mesh", None),
        ),
        out_specs=P("mesh", "state"),
        check_vma=False,
    )
```

```python
import functools
import math

import jax
import jax.numpy as jnp
from jax import lax
from jax.experimental import pallas as pl
from jax.experimental.pallas import tpu as pltpu
from jax.sharding import PartitionSpec as P

center_shift = 3.0
half_width = 4.0
f32 = jnp.float32
bf16 = jnp.bfloat16
MESH = pl.DeviceIdType.MESH


def from_behind(value, axis, steps):
    count = lax.axis_size(axis)
    first, last = (max(0, -steps), min(count, count - steps))
    return lax.ppermute(value, axis, [(source, source + steps) for source in range(first, last)])


def matmul(left, right):
    return jnp.dot(left, right, precision=lax.Precision.HIGHEST, preferred_element_type=jnp.float32)


def per_device(states_in, rotation, stiffness, potential, cell_nodes, shared_rows, shared_count):
    block_cols = states_in.shape[1]
    rotated = matmul(lax.all_gather(states_in, "state", axis=1, tiled=True), rotation)
    grid_side = math.isqrt(lax.axis_size("mesh"))
    row_mask = (jnp.arange(shared_rows.shape[1])[None, :] < shared_count[0][:, None]).astype(
        jnp.float32
    )

    def trade(values, send_slot, recv_slot, offset):
        block = values[shared_rows[send_slot]] * row_mask[send_slot][:, None]
        arrived = from_behind(block, "mesh", offset)
        return arrived * row_mask[recv_slot][:, None]

    def operator(field):
        gathered = field[cell_nodes]
        product = jnp.einsum("ij,cjs->cis", stiffness[0], gathered, precision=lax.Precision.HIGHEST)
        local = (
            jnp.zeros_like(field).at[cell_nodes.reshape(-1)].add(product.reshape(-1, block_cols))
        )
        from_next = trade(local, 1, 0, -grid_side)
        from_prev = trade(local, 0, 1, grid_side)
        sectioned = local.at[shared_rows[0]].add(from_next).at[shared_rows[1]].add(from_prev)
        from_right = trade(sectioned, 3, 2, -1)
        from_left = trade(sectioned, 2, 3, 1)
        assembled = sectioned.at[shared_rows[2]].add(from_right).at[shared_rows[3]].add(from_left)
        return assembled + potential[:, None] * field

    current = (operator(rotated) - center_shift * rotated) / half_width
    applied = operator(current)
    following = 2.0 * (applied - center_shift * current) / half_width - rotated
    return following


def up(size, unit):
    return -(-size // unit) * unit


def dot(left, right):
    return jnp.dot(left, right, preferred_element_type=f32)


def split(value):
    high = value.astype(bf16)
    return high, (value - high.astype(f32)).astype(bf16)


def dot3(lh, ll, rh, rl):
    return dot(lh, rh) + (dot(lh, rl) + dot(ll, rh))


def dot2(left, rh, rl):
    return dot(left, rh) + dot(left, rl)


def one_hot(left, right):
    return jnp.where(left == right, 1.0, 0.0).astype(bf16)


def one_hot_used(left, right):
    return jnp.where((left == right) & (left >= 0), 1.0, 0.0).astype(bf16)


def to_column(row):
    spread = jnp.broadcast_to(row.astype(f32), (128, row.shape[1]))
    return jnp.transpose(spread)[:, 0:1].astype(jnp.int32)


def kernel(
    grid_side, near_rows, far_rows,
    x_ref, rot_ref, k_ref, pot_ref, cells_ref, lists_ref, count_ref, out_ref,
    g, rbuf, c1, kh, kl, pick, same, gh, gl, ph, pl_, bv, r3,
    pot, crow, crep, ccol, dcol, near_row, far_row, near_col, far_col,
    half_put_a, half_got_a, half_put_b, half_got_b, put_a, got_a, put_b, got_b,
    k_held, g_send, g_recv, e_send, e_recv, r_sem, k_sem,
):
    nodes = x_ref.shape[0]
    n_pad, cols = c1.shape
    half = cols // 2
    n_send = up(nodes, 8)
    mid = n_pad // 2
    tile = n_pad // 2
    cells, npc = cells_ref.shape
    stride = kh.shape[0]
    side = stride // 2
    me = lax.axis_index("state")
    part = lax.axis_index("mesh")

    def flip(index, bit):
        return index + bit * (1 - 2 * (index // bit % 2))

    sib, xs, ys = flip(me, 1), flip(me, 2), flip(me, 4)
    ds = flip(xs, 4)
    pair_a, pair_b = flip(part, grid_side), flip(part, 1)
    top, low = pl.ds(0, mid), pl.ds(mid, n_send - mid)
    whole = pl.ds(0, n_send)

    barrier = pltpu.get_barrier_semaphore()
    for target in ({"state": sib}, {"state": xs}, {"state": ys}, {"mesh": pair_a}, {"mesh": pair_b}):
        pl.semaphore_signal(barrier, inc=1, device_id=target, device_id_type=MESH)

    def load_rotation(phase):
        copies = []
        for block in range(rbuf.shape[0]):
            copy = pltpu.make_async_copy(
                rot_ref.at[pl.ds(block * cols + phase * half, half)], rbuf.at[block], r_sem.at[block]
            )
            copy.start()
            copies.append(copy)
        return copies

    last = nodes // 8 * 8

    def take(phase):
        g[phase, me, pl.ds(last, n_pad - last), :] = jnp.zeros((n_pad - last, half), f32)
        g[phase, me, pl.ds(0, nodes), :] = x_ref[:, phase * half : (phase + 1) * half]

    take(0)
    pl.semaphore_wait(barrier, 5)

    def send(phase, number, owner, rows, target):
        return pltpu.make_async_remote_copy(
            src_ref=g.at[phase, owner, rows],
            dst_ref=g.at[phase, owner, rows],
            send_sem=g_send.at[phase, number],
            recv_sem=g_recv.at[phase, number],
            device_id={"state": target},
            device_id_type=MESH,
        )

    def plan(phase):
        return [
            send(phase, 0, me, top, xs),
            send(phase, 1, me, low, xs),
            send(phase, 2, ys, low, xs),
            send(phase, 3, me, low, ys),
            send(phase, 4, me, top, ys),
            send(phase, 5, xs, top, ys),
            send(phase, 6, me, whole, sib),
            send(phase, 7, xs, top, sib),
            send(phase, 8, xs, low, sib),
            send(phase, 9, ys, low, sib),
            send(phase, 10, ys, top, sib),
            send(phase, 11, ds, low, sib),
            send(phase, 12, ds, top, sib),
        ]

    plans = [plan(0), plan(1)]

    def begin(phase, *numbers):
        for number in numbers:
            plans[phase][number].start()

    def pass_on(phase, number, *onward):
        plans[phase][number].wait_recv()
        begin(phase, *onward)

    def pass_first(phase):
        pass_on(phase, 3, 2, 9)
        pass_on(phase, 0, 5, 7)

    def pass_second(phase):
        pass_on(phase, 1, 8)
        pass_on(phase, 4, 10)

    def pass_third(phase):
        pass_on(phase, 2, 11)
        pass_on(phase, 5, 12)

    def arrived(phase, *numbers):
        for number in numbers:
            plans[phase][number].wait_recv()

    begin(0, 0, 3, 6)
    k_copy = pltpu.make_async_copy(k_ref, k_held, k_sem.at[0])
    k_copy.start()
    rotation_copies = load_rotation(0)
    take(1)

    def tiles(count, size, body):
        def step(index, carry):
            body(pl.ds(pl.multiple_of(index * size, 32), size))
            return carry

        lax.fori_loop(0, count // size, step, 0)

    pot[...] = jnp.zeros(pot.shape, f32)
    pot[:, 0:nodes] = pot_ref[...].reshape(1, nodes)
    crow[...] = jnp.full(crow.shape, -1, jnp.int32)
    for cell in range(cells):
        crow[:, cell * stride : cell * stride + npc] = cells_ref[cell : cell + 1, :]
    near_row[...] = jnp.full(near_row.shape, -1, jnp.int32)
    far_row[...] = jnp.full(far_row.shape, -1, jnp.int32)
    for row_ref, offset, place in ((near_row, 0, part // grid_side), (far_row, 2, part % grid_side)):
        size = near_rows if row_ref is near_row else far_rows
        ids = lax.broadcasted_iota(jnp.int32, (1, size), 1)
        second = place == 1
        listed = jnp.where(
            second, lists_ref[offset + 1 : offset + 2, 0:size], lists_ref[offset : offset + 1, 0:size]
        )
        count = jnp.where(second, count_ref[0, offset + 1], count_ref[0, offset])
        row_ref[:, 0:size] = jnp.where(ids < count, listed, -1)
    near_col[...] = to_column(near_row[...])[0 : near_col.shape[0]]
    far_col[...] = to_column(far_row[...])[0 : far_col.shape[0]]
    ccol[...] = to_column(crow[...])

    k_copy.wait()
    for first in range(0, stride, cols):
        width = min(cols, stride - first)
        used = min(npc - first, width)
        out_ref[0:stride, 0:width] = jnp.zeros((stride, width), f32)
        out_ref[0:npc, 0:used] = k_held[:, 0, first : first + used]
        span = slice(first, first + width)
        kh[:, span], kl[:, span] = split(out_ref[0:stride, 0:width])

    def pick_body(rows):
        ids = lax.broadcasted_iota(jnp.int32, (side, n_pad), 1)
        here = ccol[rows, :] == ids
        pick[rows, :] = jnp.where(here, 1.0, 0.0).astype(bf16)
        dcol[rows, :] = jnp.sum(jnp.where(here, pot[...], 0.0), axis=1, keepdims=True) - center_shift

    tiles(cells * stride, side, pick_body)
    crep[...] = crow[...]
    pairs = [(one, two) for one in range(cells) for two in range(cells) if one != two]
    for index, (one, two) in enumerate(pairs):
        left = ccol[one * stride : (one + 1) * stride, :]
        span = slice(two * stride, (two + 1) * stride)
        both = one_hot_used(left, crow[:, span])
        same[index] = both
        if one < two:
            taken = jnp.max(both.astype(f32), axis=0, keepdims=True)
            crep[:, span] = jnp.where(taken > 0.5, -1, crep[:, span])

    begin(0, 1, 4)

    def rotate(phase, owner, total, fresh=False):
        high, rest = split(rbuf[owner])
        r3[0:half], r3[half : 2 * half], r3[2 * half :] = high, rest, high

        def body(rows):
            high, rest = split(g[phase, owner, rows, :])
            value = dot(jnp.concatenate([high, high, rest], axis=1), r3[...])
            total[rows, :] = value if fresh else total[rows, :] + value

        tiles(n_pad, tile, body)

    buffers = (
        ((half_put_a, half_got_a, pair_a), (half_put_b, half_got_b, pair_b)),
        ((put_a, got_a, pair_a), (put_b, got_b, pair_b)),
    )

    def trade(field, number, which):
        put, got, pair = buffers[field][which]
        return pltpu.make_async_remote_copy(
            src_ref=put.at[number],
            dst_ref=got.at[number],
            send_sem=e_send.at[which, 2 * field + number],
            recv_sem=e_recv.at[which, 2 * field + number],
            device_id={"mesh": pair},
            device_id_type=MESH,
        )

    def hold(field, high_ref, rest_ref, rows, value):
        high, rest = split(value)
        if field:
            high_ref[rows, :], rest_ref[rows, :] = high, rest
        else:
            high_ref[rows, 0:half], high_ref[rows, half:] = high, rest

    def fold(value):
        return value[:, 0:half] + value[:, half:]

    def times(field, left, high_ref, rest_ref, rows):
        if field:
            return dot2(left, high_ref[rows, :], rest_ref[rows, :])
        return fold(dot(left, high_ref[rows, :]))

    def times_value(field, left, value):
        high, rest = split(value)
        if field:
            return dot2(left, high, rest)
        return fold(dot(left, jnp.concatenate([high, rest], axis=1)))

    def width(field):
        return slice(0, cols if field else half)

    def enter(field, read):
        def split_body(rows):
            hold(field, ph, pl_, rows, read(rows))

        tiles(n_pad, tile, split_body)

        def body(rows):
            gh[rows, :] = dot(pick[rows, :], ph[0:n_pad, :]).astype(bf16)
            if field:
                gl[rows, :] = dot(pick[rows, :], pl_[0:n_pad, :]).astype(bf16)

        tiles(cells * stride, side, body)

    def product(field, number):
        for cell in range(cells):
            span = slice(cell * stride, (cell + 1) * stride)

            def body(rows):
                here = pl.ds(pl.multiple_of(rows.start + cell * stride, 32), side)
                value = times(field, kh[rows, :], gh, gl, span)
                value = value + dot(kl[rows, :], gh[span, width(field)])
                hold(field, ph, pl_, here, value)
                if field:
                    held = gh[here, :].astype(f32) + gl[here, :].astype(f32)
                else:
                    held = fold(gh[here, :].astype(f32))
                bv[here, width(field)] = value + dcol[here, :] * held

            tiles(stride, side, body)
        every = slice(0, cells * stride)
        for which, col in ((0, near_col), (1, far_col)):
            picked = times(field, one_hot_used(col[...], crow[...]), ph, pl_, every)
            buffers[field][which][0][number] = picked
            if which == 0:
                trade(field, number, 0).start()

    def couple(field):
        for index, (one, two) in enumerate(pairs):
            span = slice(two * stride, (two + 1) * stride)

            def body(rows):
                here = pl.ds(pl.multiple_of(rows.start + one * stride, 32), side)
                value = times(field, same[index, rows, :], ph, pl_, span)
                bv[here, width(field)] = bv[here, width(field)] + value

            tiles(stride, side, body)

    def link(field, number):
        trade(field, number, 0).wait_recv()
        corner = one_hot_used(far_col[...], near_row[:, 0 : near_col.shape[0]])
        got, put = buffers[field][0][1], buffers[field][1][0]
        put[number] = put[number] + times_value(field, corner, got[number])
        trade(field, number, 1).start()

    def finish(field, number):
        trade(field, number, 1).wait_recv()
        near_got, far_got = buffers[field][0][1], buffers[field][1][1]

        def body(rows):
            near = one_hot_used(ccol[rows, :], near_row[:, 0 : near_col.shape[0]])
            far = one_hot_used(ccol[rows, :], far_row[:, 0 : far_col.shape[0]])
            value = bv[rows, width(field)] + times_value(field, near, near_got[number])
            value = value + times_value(field, far, far_got[number])
            hold(field, gh, gl, rows, value * (1.0 / half_width))

        tiles(cells * stride, side, body)

    def leave(field, write):
        size = tile // 2

        def body(rows):
            ids = lax.broadcasted_iota(jnp.int32, (size, crep.shape[1]), 0) + rows.start
            write(rows, times(field, one_hot(ids, crep[...]), gh, gl, slice(0, cells * stride)))

        tiles(n_pad, size, body)

    enter(0, lambda rows: g[1, me, rows, :])
    product(0, 0)
    couple(0)
    for copy in rotation_copies:
        copy.wait()
    rotate(0, me, c1, fresh=True)
    link(0, 0)
    arrived(0, 6)
    rotate(0, sib, c1)
    finish(0, 0)
    product(0, 1)
    couple(0)
    pass_first(0)
    link(0, 1)
    pass_second(0)
    rotate(0, xs, c1)
    finish(0, 1)

    def leave_half(rows, value):
        g[1, me, rows, :] = 2.0 * value - g[1, me, rows, :]

    leave(0, leave_half)
    begin(1, 0, 3, 6)
    rotate(0, ys, c1)
    arrived(0, 7, 8)
    rotate(0, flip(xs, 1), c1)
    arrived(0, 9, 10)
    rotate(0, flip(ys, 1), c1)
    pass_third(0)
    rotate(0, ds, c1)
    arrived(0, 11, 12)
    rotate(0, flip(ds, 1), c1)
    rotation_copies = load_rotation(1)
    c1[pl.ds(n_send, n_pad - n_send), :] = jnp.zeros((n_pad - n_send, cols), f32)

    enter(1, lambda rows: c1[rows, :])
    begin(1, 1, 4)
    product(1, 0)
    couple(1)
    for copy in rotation_copies:
        copy.wait()
    rotate(1, me, out_ref, fresh=True)
    link(1, 0)
    pass_first(1)
    arrived(1, 6)
    rotate(1, sib, out_ref)
    finish(1, 0)
    product(1, 1)
    couple(1)
    link(1, 1)
    pass_second(1)
    rotate(1, xs, out_ref)
    rotate(1, ys, out_ref)
    finish(1, 1)

    def leave_whole(rows, value):
        out_ref[rows, :] = out_ref[rows, :] + (2.0 * value - c1[rows, :])

    leave(1, leave_whole)
    arrived(1, 7, 8)
    rotate(1, flip(xs, 1), out_ref)
    arrived(1, 9, 10)
    rotate(1, flip(ys, 1), out_ref)
    pass_third(1)
    rotate(1, ds, out_ref)
    arrived(1, 11, 12)
    rotate(1, flip(ds, 1), out_ref)
    for moves in plans:
        for move in moves:
            move.wait_send()
    for field in range(2):
        for number in range(2):
            for which in range(2):
                trade(field, number, which).wait_send()


def square_device(states_in, rotation, stiffness, potential, cell_nodes, shared_rows, shared_count):
    nodes, cols = states_in.shape
    half = cols // 2
    blocks = lax.axis_size("state")
    n_pad = up(nodes, 128)
    cells, npc = cell_nodes.shape
    stride = up(npc, 256)
    side = round(npc ** (1 / 3))
    near_rows, far_rows = side * side, shared_rows.shape[1]
    near, far = up(near_rows, 32), up(far_rows, 32)
    grid_side = math.isqrt(lax.axis_size("mesh"))
    vmem = pl.BlockSpec(memory_space=pltpu.VMEM)
    smem = pl.BlockSpec(memory_space=pltpu.SMEM)
    held = pl.BlockSpec(memory_space=pl.ANY)
    scratch = [
        pltpu.VMEM((2, blocks, n_pad, half), f32),
        pltpu.VMEM((blocks, half, cols), f32),
        pltpu.VMEM((n_pad, cols), f32),
        pltpu.VMEM((stride, stride), bf16),
        pltpu.VMEM((stride, stride), bf16),
        pltpu.VMEM((cells * stride, n_pad), bf16),
        pltpu.VMEM((cells * (cells - 1), stride, stride), bf16),
        pltpu.VMEM((cells * stride, cols), bf16),
        pltpu.VMEM((cells * stride, cols), bf16),
        pltpu.VMEM((cells * stride, cols), bf16),
        pltpu.VMEM((cells * stride, cols), bf16),
        pltpu.VMEM((cells * stride, cols), f32),
        pltpu.VMEM((3 * half, cols), bf16),
        pltpu.VMEM((1, n_pad), f32),
        pltpu.VMEM((1, cells * stride), jnp.int32),
        pltpu.VMEM((1, cells * stride), jnp.int32),
        pltpu.VMEM((cells * stride, 1), jnp.int32),
        pltpu.VMEM((cells * stride, 1), f32),
        pltpu.VMEM((1, up(near, 128)), jnp.int32),
        pltpu.VMEM((1, up(far, 128)), jnp.int32),
        pltpu.VMEM((near, 1), jnp.int32),
        pltpu.VMEM((far, 1), jnp.int32),
        pltpu.VMEM((2, near, half), f32),
        pltpu.VMEM((2, near, half), f32),
        pltpu.VMEM((2, far, half), f32),
        pltpu.VMEM((2, far, half), f32),
        pltpu.VMEM((2, near, cols), f32),
        pltpu.VMEM((2, near, cols), f32),
        pltpu.VMEM((2, far, cols), f32),
        pltpu.VMEM((2, far, cols), f32),
        pltpu.VMEM((npc, 1, npc), f32),
        pltpu.SemaphoreType.DMA((2, 13)),
        pltpu.SemaphoreType.DMA((2, 13)),
        pltpu.SemaphoreType.DMA((2, 4)),
        pltpu.SemaphoreType.DMA((2, 4)),
        pltpu.SemaphoreType.DMA((blocks,)),
        pltpu.SemaphoreType.DMA((1,)),
    ]
    padded = pl.pallas_call(
        functools.partial(kernel, grid_side, near_rows, far_rows),
        out_shape=jax.ShapeDtypeStruct((n_pad, cols), f32),
        in_specs=[vmem, held, held, vmem, vmem, vmem, smem],
        out_specs=vmem,
        scratch_shapes=scratch,
        compiler_params=pltpu.CompilerParams(
            collective_id=0, has_side_effects=True, vmem_limit_bytes=64 * 1024 * 1024
        ),
    )(
        states_in,
        rotation,
        jnp.transpose(stiffness, (1, 0, 2)),
        potential,
        cell_nodes,
        shared_rows,
        shared_count,
    )
    return padded[:nodes]


def solution(mesh):
    squares = mesh.shape["state"] == 2 * 2 * 2 and mesh.shape["mesh"] == 2 * 2
    return jax.shard_map(
        square_device if squares else per_device,
        mesh=mesh,
        in_specs=(
            P("mesh", "state"),
            P(None, "state"),
            P("mesh", None, None),
            P("mesh"),
            P("mesh", None),
            P("mesh", None),
            P("mesh", None),
        ),
        out_specs=P("mesh", "state"),
        check_vma=False,
    )
```

```python
import functools
import math

import jax
import jax.numpy as jnp
from jax import lax
from jax.experimental import pallas as pl
from jax.experimental.pallas import tpu as pltpu
from jax.sharding import PartitionSpec as P

center_shift = 3.0
half_width = 4.0
f32 = jnp.float32
bf16 = jnp.bfloat16
MESH = pl.DeviceIdType.MESH


def from_behind(value, axis, steps):
    count = lax.axis_size(axis)
    first, last = (max(0, -steps), min(count, count - steps))
    return lax.ppermute(value, axis, [(source, source + steps) for source in range(first, last)])


def matmul(left, right):
    return jnp.dot(left, right, precision=lax.Precision.HIGHEST, preferred_element_type=jnp.float32)


def per_device(states_in, rotation, stiffness, potential, cell_nodes, shared_rows, shared_count):
    block_cols = states_in.shape[1]
    rotated = matmul(lax.all_gather(states_in, "state", axis=1, tiled=True), rotation)
    grid_side = math.isqrt(lax.axis_size("mesh"))
    row_mask = (jnp.arange(shared_rows.shape[1])[None, :] < shared_count[0][:, None]).astype(
        jnp.float32
    )

    def trade(values, send_slot, recv_slot, offset):
        block = values[shared_rows[send_slot]] * row_mask[send_slot][:, None]
        arrived = from_behind(block, "mesh", offset)
        return arrived * row_mask[recv_slot][:, None]

    def operator(field):
        gathered = field[cell_nodes]
        product = jnp.einsum("ij,cjs->cis", stiffness[0], gathered, precision=lax.Precision.HIGHEST)
        local = (
            jnp.zeros_like(field).at[cell_nodes.reshape(-1)].add(product.reshape(-1, block_cols))
        )
        from_next = trade(local, 1, 0, -grid_side)
        from_prev = trade(local, 0, 1, grid_side)
        sectioned = local.at[shared_rows[0]].add(from_next).at[shared_rows[1]].add(from_prev)
        from_right = trade(sectioned, 3, 2, -1)
        from_left = trade(sectioned, 2, 3, 1)
        assembled = sectioned.at[shared_rows[2]].add(from_right).at[shared_rows[3]].add(from_left)
        return assembled + potential[:, None] * field

    current = (operator(rotated) - center_shift * rotated) / half_width
    applied = operator(current)
    following = 2.0 * (applied - center_shift * current) / half_width - rotated
    return following


def up(size, unit):
    return -(-size // unit) * unit


def dot(left, right):
    return jnp.dot(left, right, preferred_element_type=f32)


def split(value):
    high = value.astype(bf16)
    return high, (value - high.astype(f32)).astype(bf16)


def dot3(lh, ll, rh, rl):
    return dot(lh, rh) + (dot(lh, rl) + dot(ll, rh))


def dot2(left, rh, rl):
    return dot(left, rh) + dot(left, rl)


def one_hot(left, right):
    return jnp.where(left == right, 1.0, 0.0).astype(bf16)


def one_hot_used(left, right):
    return jnp.where((left == right) & (left >= 0), 1.0, 0.0).astype(bf16)


def to_column(row):
    spread = jnp.broadcast_to(row.astype(f32), (128, row.shape[1]))
    return jnp.transpose(spread)[:, 0:1].astype(jnp.int32)


def kernel(
    grid_side, near_rows, far_rows,
    x_ref, rot_ref, k_ref, pot_ref, cells_ref, lists_ref, count_ref, out_ref,
    g, rbuf, c1, kh, kl, pick, same, gh, gl, ph, pl_, bv, r3,
    pot, crow, crep, ccol, dcol, near_row, far_row, near_col, far_col,
    half_put_a, half_got_a, half_put_b, half_got_b, put_a, got_a, put_b, got_b,
    k_held, g_send, g_recv, e_send, e_recv, r_sem, k_sem,
):
    nodes = x_ref.shape[0]
    n_pad, cols = c1.shape
    half = cols // 2
    n_send = up(nodes, 8)
    mid = n_pad // 2
    tile = n_pad // 2
    cells, npc = cells_ref.shape
    stride = kh.shape[0]
    side = stride // 2
    me = lax.axis_index("state")
    part = lax.axis_index("mesh")

    def flip(index, bit):
        return index + bit * (1 - 2 * (index // bit % 2))

    sib, xs, ys = flip(me, 1), flip(me, 2), flip(me, 4)
    ds = flip(xs, 4)
    pair_a, pair_b = flip(part, grid_side), flip(part, 1)
    top, low = pl.ds(0, mid), pl.ds(mid, n_send - mid)
    whole = pl.ds(0, n_send)

    barrier = pltpu.get_barrier_semaphore()
    for target in ({"state": sib}, {"state": xs}, {"state": ys}, {"mesh": pair_a}, {"mesh": pair_b}):
        pl.semaphore_signal(barrier, inc=1, device_id=target, device_id_type=MESH)

    def load_block(phase, block):
        rows = pl.ds(pl.multiple_of(block * cols + phase * half, half), half)
        copy = pltpu.make_async_copy(rot_ref.at[rows], rbuf.at[block], r_sem.at[block])
        copy.start()
        return copy

    def load_rotation(phase):
        return [load_block(phase, block) for block in range(rbuf.shape[0])]

    last = nodes // 8 * 8

    def take(phase):
        g[phase, me, pl.ds(last, n_pad - last), :] = jnp.zeros((n_pad - last, half), f32)
        g[phase, me, pl.ds(0, nodes), :] = x_ref[:, phase * half : (phase + 1) * half]

    take(0)
    pl.semaphore_wait(barrier, 5)

    def send(phase, number, owner, rows, target):
        return pltpu.make_async_remote_copy(
            src_ref=g.at[phase, owner, rows],
            dst_ref=g.at[phase, owner, rows],
            send_sem=g_send.at[phase, number],
            recv_sem=g_recv.at[phase, number],
            device_id={"state": target},
            device_id_type=MESH,
        )

    def plan(phase):
        return [
            send(phase, 0, me, top, xs),
            send(phase, 1, me, low, xs),
            send(phase, 2, ys, low, xs),
            send(phase, 3, me, low, ys),
            send(phase, 4, me, top, ys),
            send(phase, 5, xs, top, ys),
            send(phase, 6, me, whole, sib),
            send(phase, 7, xs, top, sib),
            send(phase, 8, xs, low, sib),
            send(phase, 9, ys, low, sib),
            send(phase, 10, ys, top, sib),
            send(phase, 11, ds, low, sib),
            send(phase, 12, ds, top, sib),
        ]

    plans = [plan(0), plan(1)]

    def begin(phase, *numbers):
        for number in numbers:
            plans[phase][number].start()

    def pass_on(phase, number, *onward):
        plans[phase][number].wait_recv()
        begin(phase, *onward)

    def pass_first(phase):
        pass_on(phase, 3, 2, 9)
        pass_on(phase, 0, 5, 7)

    def pass_second(phase):
        pass_on(phase, 1, 8)
        pass_on(phase, 4, 10)

    def pass_third(phase):
        pass_on(phase, 2, 11)
        pass_on(phase, 5, 12)

    def arrived(phase, *numbers):
        for number in numbers:
            plans[phase][number].wait_recv()

    begin(0, 0, 3, 6)
    k_copy = pltpu.make_async_copy(k_ref, k_held, k_sem.at[0])
    k_copy.start()
    rotation_copies = load_rotation(0)
    take(1)

    def tiles(count, size, body):
        def step(index, carry):
            body(pl.ds(pl.multiple_of(index * size, 32), size))
            return carry

        lax.fori_loop(0, count // size, step, 0)

    pot[...] = jnp.zeros(pot.shape, f32)
    pot[:, 0:nodes] = pot_ref[...].reshape(1, nodes)
    crow[...] = jnp.full(crow.shape, -1, jnp.int32)
    for cell in range(cells):
        crow[:, cell * stride : cell * stride + npc] = cells_ref[cell : cell + 1, :]
    near_row[...] = jnp.full(near_row.shape, -1, jnp.int32)
    far_row[...] = jnp.full(far_row.shape, -1, jnp.int32)
    for row_ref, offset, place in ((near_row, 0, part // grid_side), (far_row, 2, part % grid_side)):
        size = near_rows if row_ref is near_row else far_rows
        ids = lax.broadcasted_iota(jnp.int32, (1, size), 1)
        second = place == 1
        listed = jnp.where(
            second, lists_ref[offset + 1 : offset + 2, 0:size], lists_ref[offset : offset + 1, 0:size]
        )
        count = jnp.where(second, count_ref[0, offset + 1], count_ref[0, offset])
        row_ref[:, 0:size] = jnp.where(ids < count, listed, -1)
    near_col[...] = to_column(near_row[...])[0 : near_col.shape[0]]
    far_col[...] = to_column(far_row[...])[0 : far_col.shape[0]]
    ccol[...] = to_column(crow[...])

    k_copy.wait()
    for first in range(0, stride, cols):
        width = min(cols, stride - first)
        used = min(npc - first, width)
        out_ref[0:stride, 0:width] = jnp.zeros((stride, width), f32)
        out_ref[0:npc, 0:used] = k_held[:, 0, first : first + used]
        span = slice(first, first + width)
        kh[:, span], kl[:, span] = split(out_ref[0:stride, 0:width])

    def pick_body(rows):
        ids = lax.broadcasted_iota(jnp.int32, (side, n_pad), 1)
        here = ccol[rows, :] == ids
        pick[rows, :] = jnp.where(here, 1.0, 0.0).astype(bf16)
        dcol[rows, :] = jnp.sum(jnp.where(here, pot[...], 0.0), axis=1, keepdims=True) - center_shift

    tiles(cells * stride, side, pick_body)
    crep[...] = crow[...]
    pairs = [(one, two) for one in range(cells) for two in range(cells) if one != two]
    for index, (one, two) in enumerate(pairs):
        left = ccol[one * stride : (one + 1) * stride, :]
        span = slice(two * stride, (two + 1) * stride)
        both = one_hot_used(left, crow[:, span])
        same[index] = both
        if one < two:
            taken = jnp.max(both.astype(f32), axis=0, keepdims=True)
            crep[:, span] = jnp.where(taken > 0.5, -1, crep[:, span])

    begin(0, 1, 4)

    def rotate(phase, owner, total, fresh=False):
        high, rest = split(rbuf[owner])
        r3[0:half], r3[half : 2 * half], r3[2 * half :] = high, rest, high

        def body(rows):
            high, rest = split(g[phase, owner, rows, :])
            value = dot(jnp.concatenate([high, high, rest], axis=1), r3[...])
            total[rows, :] = value if fresh else total[rows, :] + value

        tiles(n_pad, tile, body)

    buffers = (
        ((half_put_a, half_got_a, pair_a), (half_put_b, half_got_b, pair_b)),
        ((put_a, got_a, pair_a), (put_b, got_b, pair_b)),
    )

    def trade(field, number, which):
        put, got, pair = buffers[field][which]
        return pltpu.make_async_remote_copy(
            src_ref=put.at[number],
            dst_ref=got.at[number],
            send_sem=e_send.at[which, 2 * field + number],
            recv_sem=e_recv.at[which, 2 * field + number],
            device_id={"mesh": pair},
            device_id_type=MESH,
        )

    def hold(field, high_ref, rest_ref, rows, value):
        high, rest = split(value)
        if field:
            high_ref[rows, :], rest_ref[rows, :] = high, rest
        else:
            high_ref[rows, 0:half], high_ref[rows, half:] = high, rest

    def fold(value):
        return value[:, 0:half] + value[:, half:]

    def times(field, left, high_ref, rest_ref, rows):
        if field:
            return dot2(left, high_ref[rows, :], rest_ref[rows, :])
        return fold(dot(left, high_ref[rows, :]))

    def times_value(field, left, value):
        high, rest = split(value)
        if field:
            return dot2(left, high, rest)
        return fold(dot(left, jnp.concatenate([high, rest], axis=1)))

    def width(field):
        return slice(0, cols if field else half)

    def enter(field, read):
        def split_body(rows):
            hold(field, ph, pl_, rows, read(rows))

        tiles(n_pad, tile, split_body)

        def body(rows):
            gh[rows, :] = dot(pick[rows, :], ph[0:n_pad, :]).astype(bf16)
            if field:
                gl[rows, :] = dot(pick[rows, :], pl_[0:n_pad, :]).astype(bf16)

        tiles(cells * stride, side, body)

    def product(field, number):
        for cell in range(cells):
            span = slice(cell * stride, (cell + 1) * stride)

            def body(rows):
                here = pl.ds(pl.multiple_of(rows.start + cell * stride, 32), side)
                value = times(field, kh[rows, :], gh, gl, span)
                value = value + dot(kl[rows, :], gh[span, width(field)])
                hold(field, ph, pl_, here, value)
                if field:
                    held = gh[here, :].astype(f32) + gl[here, :].astype(f32)
                else:
                    held = fold(gh[here, :].astype(f32))
                bv[here, width(field)] = value + dcol[here, :] * held

            tiles(stride, side, body)
        every = slice(0, cells * stride)
        for which, col in ((0, near_col), (1, far_col)):
            picked = times(field, one_hot_used(col[...], crow[...]), ph, pl_, every)
            buffers[field][which][0][number] = picked
            if which == 0:
                trade(field, number, 0).start()

    def couple(field):
        for index, (one, two) in enumerate(pairs):
            span = slice(two * stride, (two + 1) * stride)

            def body(rows):
                here = pl.ds(pl.multiple_of(rows.start + one * stride, 32), side)
                value = times(field, same[index, rows, :], ph, pl_, span)
                bv[here, width(field)] = bv[here, width(field)] + value

            tiles(stride, side, body)

    def link(field, number):
        trade(field, number, 0).wait_recv()
        corner = one_hot_used(far_col[...], near_row[:, 0 : near_col.shape[0]])
        got, put = buffers[field][0][1], buffers[field][1][0]
        put[number] = put[number] + times_value(field, corner, got[number])
        trade(field, number, 1).start()

    def finish(field, number):
        trade(field, number, 1).wait_recv()
        near_got, far_got = buffers[field][0][1], buffers[field][1][1]

        def body(rows):
            near = one_hot_used(ccol[rows, :], near_row[:, 0 : near_col.shape[0]])
            far = one_hot_used(ccol[rows, :], far_row[:, 0 : far_col.shape[0]])
            value = bv[rows, width(field)] + times_value(field, near, near_got[number])
            value = value + times_value(field, far, far_got[number])
            hold(field, gh, gl, rows, value * (1.0 / half_width))

        tiles(cells * stride, side, body)

    def leave(field, write):
        size = tile // 2

        def body(rows):
            ids = lax.broadcasted_iota(jnp.int32, (size, crep.shape[1]), 0) + rows.start
            write(rows, times(field, one_hot(ids, crep[...]), gh, gl, slice(0, cells * stride)))

        tiles(n_pad, size, body)

    enter(0, lambda rows: g[1, me, rows, :])
    product(0, 0)
    couple(0)
    for copy in rotation_copies:
        copy.wait()
    rotate(0, me, c1, fresh=True)
    own_copy = load_block(1, me)
    link(0, 0)
    arrived(0, 6)
    rotate(0, sib, c1)
    finish(0, 0)
    product(0, 1)
    couple(0)
    pass_first(0)
    link(0, 1)
    pass_second(0)
    rotate(0, xs, c1)
    finish(0, 1)

    def leave_half(rows, value):
        g[1, me, rows, :] = 2.0 * value - g[1, me, rows, :]

    leave(0, leave_half)
    begin(1, 6)
    rotate(0, ys, c1)
    arrived(0, 7, 8)
    rotate(0, flip(xs, 1), c1)
    arrived(0, 9, 10)
    rotate(0, flip(ys, 1), c1)
    own_copy.wait()
    rotate(1, me, out_ref, fresh=True)
    pass_third(0)
    begin(1, 0, 3)
    rotate(0, ds, c1)
    arrived(0, 11, 12)
    rotate(0, flip(ds, 1), c1)
    rotation_copies = load_rotation(1)
    c1[pl.ds(n_send, n_pad - n_send), :] = jnp.zeros((n_pad - n_send, cols), f32)

    enter(1, lambda rows: c1[rows, :])
    product(1, 0)
    begin(1, 1, 4)
    couple(1)
    for copy in rotation_copies:
        copy.wait()
    link(1, 0)
    arrived(1, 6)
    rotate(1, sib, out_ref)
    finish(1, 0)
    product(1, 1)
    pass_first(1)
    couple(1)
    link(1, 1)
    pass_second(1)
    rotate(1, xs, out_ref)
    rotate(1, ys, out_ref)
    finish(1, 1)

    def leave_whole(rows, value):
        out_ref[rows, :] = out_ref[rows, :] + (2.0 * value - c1[rows, :])

    leave(1, leave_whole)
    arrived(1, 7, 8)
    rotate(1, flip(xs, 1), out_ref)
    arrived(1, 9, 10)
    rotate(1, flip(ys, 1), out_ref)
    pass_third(1)
    rotate(1, ds, out_ref)
    arrived(1, 11, 12)
    rotate(1, flip(ds, 1), out_ref)
    for moves in plans:
        for move in moves:
            move.wait_send()
    for field in range(2):
        for number in range(2):
            for which in range(2):
                trade(field, number, which).wait_send()


def square_device(states_in, rotation, stiffness, potential, cell_nodes, shared_rows, shared_count):
    nodes, cols = states_in.shape
    half = cols // 2
    blocks = lax.axis_size("state")
    n_pad = up(nodes, 128)
    cells, npc = cell_nodes.shape
    stride = up(npc, 256)
    side = round(npc ** (1 / 3))
    near_rows, far_rows = side * side, shared_rows.shape[1]
    near, far = up(near_rows, 32), up(far_rows, 32)
    grid_side = math.isqrt(lax.axis_size("mesh"))
    vmem = pl.BlockSpec(memory_space=pltpu.VMEM)
    smem = pl.BlockSpec(memory_space=pltpu.SMEM)
    held = pl.BlockSpec(memory_space=pl.ANY)
    scratch = [
        pltpu.VMEM((2, blocks, n_pad, half), f32),
        pltpu.VMEM((blocks, half, cols), f32),
        pltpu.VMEM((n_pad, cols), f32),
        pltpu.VMEM((stride, stride), bf16),
        pltpu.VMEM((stride, stride), bf16),
        pltpu.VMEM((cells * stride, n_pad), bf16),
        pltpu.VMEM((cells * (cells - 1), stride, stride), bf16),
        pltpu.VMEM((cells * stride, cols), bf16),
        pltpu.VMEM((cells * stride, cols), bf16),
        pltpu.VMEM((cells * stride, cols), bf16),
        pltpu.VMEM((cells * stride, cols), bf16),
        pltpu.VMEM((cells * stride, cols), f32),
        pltpu.VMEM((3 * half, cols), bf16),
        pltpu.VMEM((1, n_pad), f32),
        pltpu.VMEM((1, cells * stride), jnp.int32),
        pltpu.VMEM((1, cells * stride), jnp.int32),
        pltpu.VMEM((cells * stride, 1), jnp.int32),
        pltpu.VMEM((cells * stride, 1), f32),
        pltpu.VMEM((1, up(near, 128)), jnp.int32),
        pltpu.VMEM((1, up(far, 128)), jnp.int32),
        pltpu.VMEM((near, 1), jnp.int32),
        pltpu.VMEM((far, 1), jnp.int32),
        pltpu.VMEM((2, near, half), f32),
        pltpu.VMEM((2, near, half), f32),
        pltpu.VMEM((2, far, half), f32),
        pltpu.VMEM((2, far, half), f32),
        pltpu.VMEM((2, near, cols), f32),
        pltpu.VMEM((2, near, cols), f32),
        pltpu.VMEM((2, far, cols), f32),
        pltpu.VMEM((2, far, cols), f32),
        pltpu.VMEM((npc, 1, npc), f32),
        pltpu.SemaphoreType.DMA((2, 13)),
        pltpu.SemaphoreType.DMA((2, 13)),
        pltpu.SemaphoreType.DMA((2, 4)),
        pltpu.SemaphoreType.DMA((2, 4)),
        pltpu.SemaphoreType.DMA((blocks,)),
        pltpu.SemaphoreType.DMA((1,)),
    ]
    padded = pl.pallas_call(
        functools.partial(kernel, grid_side, near_rows, far_rows),
        out_shape=jax.ShapeDtypeStruct((n_pad, cols), f32),
        in_specs=[vmem, held, held, vmem, vmem, vmem, smem],
        out_specs=vmem,
        scratch_shapes=scratch,
        compiler_params=pltpu.CompilerParams(
            collective_id=0, has_side_effects=True, vmem_limit_bytes=64 * 1024 * 1024
        ),
    )(
        states_in,
        rotation,
        jnp.transpose(stiffness, (1, 0, 2)),
        potential,
        cell_nodes,
        shared_rows,
        shared_count,
    )
    return padded[:nodes]


def solution(mesh):
    squares = mesh.shape["state"] == 2 * 2 * 2 and mesh.shape["mesh"] == 2 * 2
    return jax.shard_map(
        square_device if squares else per_device,
        mesh=mesh,
        in_specs=(
            P("mesh", "state"),
            P(None, "state"),
            P("mesh", None, None),
            P("mesh"),
            P("mesh", None),
            P("mesh", None),
            P("mesh", None),
        ),
        out_specs=P("mesh", "state"),
        check_vma=False,
    )
```
